256 devices in a mesh: row: 32 (over z_lo, y, core), aisle: 8 (over z_hi, x).
Axes of the slice: x: 4, y: 4, z: 8 (z_hi: 2, z_lo: 4; z = z_hi * 4 + z_lo), core: 2. Of those that a mesh axis runs over, the one named last changes fastest.
Arguments:
- tokens: bfloat16 [96, 128, 4, 512], P('row', 'aisle'), may hold values from -8 to 8
- ln_gain: float32 [512], replicated, may hold values from 0.1 to 1.9
- w_qkv: bfloat16 [512, 1536], replicated, may hold values from -2 to 2
- w_out: bfloat16 [512, 512], replicated, may hold values from -0.75 to 0.75
- w_rec: bfloat16 [512, 6912], replicated, may hold values from -0.25 to 0.25
- solid_top: int32 [768, 1024], P('row', 'aisle'), may hold values from -32 to 32
Outputs:
- flow_field: bfloat16 [4, 32, 768, 1024], P(None, None, 'row', 'aisle')
The draws below stay inside these ranges and needn't reach their ends.
All inputs are finite; a program needn't handle non-finite values.
Results may differ from the reference program's by a relative error of at most 0.0075.
Values may be sent and summed in bfloat16 or wider, within the bound.
A program may use at most 128 MiB of HBM per device.

```python
import math
import jax
import jax.numpy as jnp
from jax import lax

D = 512
HEADS = 8
CHANNELS = 4
AD = 16
HEIGHT = 4
ROWS = 96
AISLE = 128
XC = 768
YC = 1024
ZC = 32
N_AISLE = 8


def draw_tokens(key, part):
    full_shape = (ROWS, AISLE, HEIGHT, D)
    drawn = jax.random.normal(key, full_shape, jnp.float32)
    return jnp.clip(drawn, -6.0, 6.0).astype(jnp.bfloat16)


def draw_w_qkv(key, part):
    scaled_key, value_key = jax.random.split(jax.random.fold_in(key, 5), 2)
    inverse = 1.0 / math.sqrt(D)
    paired = jax.random.normal(scaled_key, (D, 2 * D), jnp.float32) * inverse
    valued = jax.random.normal(value_key, (D, D), jnp.float32) * 2.0 * inverse
    joined = jnp.concatenate([paired, valued], axis=1)
    return jnp.clip(joined, -2.0, 2.0).astype(jnp.bfloat16)


def with_ends(values, rng, low, largest):
    dims = values.shape
    index_at = [jax.random.randint(jax.random.fold_in(rng, axis), (), 0, dims[axis]) for axis in range(len(dims))]
    values = values.at[tuple(index_at)].set(low)
    longest = dims.index(max(dims))
    index_at[longest] = (index_at[longest] + 1) % dims[longest]
    return values.at[tuple(index_at)].set(largest)


def noise(rng, dims, width, bound, held_as=jnp.bfloat16):
    return jnp.clip(width * jax.random.normal(rng, dims, jnp.float32), -bound, bound).astype(held_as)


def setup_inputs(seed: int = 0) -> dict:
    splits = jax.random.split(jax.random.key(seed), 7)
    return {
        "tokens": draw_tokens(jax.random.fold_in(splits[6], 71), 0),
        "ln_gain": jnp.clip(1.0 + 0.18 * jax.random.normal(splits[1], (D,), jnp.float32), 0.1, 1.9),
        "w_qkv": draw_w_qkv(jax.random.fold_in(splits[6], 71), 0),
        "w_out": noise(splits[3], (D, D), (D // 8) ** -0.5, 0.75),
        "w_rec": noise(splits[4], (D, 1728 * CHANNELS), D ** -0.5, 0.25),
        "solid_top": with_ends(jax.random.randint(splits[5], (XC, YC), -8 * HEIGHT, 8 * HEIGHT + 1), jax.random.fold_in(splits[5], 1), -8 * HEIGHT, 8 * HEIGHT).astype(jnp.int32),
    }


EPSILON = 1e-05

def layer_norm(values, scaling):
    widened = values.astype(jnp.float32)
    center = widened - lax.optimization_barrier(jnp.mean(widened, axis=-1, keepdims=True))
    spread = lax.optimization_barrier(jnp.mean(center * center, axis=-1, keepdims=True))
    return (center * lax.rsqrt(spread + EPSILON) * scaling).astype(jnp.bfloat16)

def attend(block):
    rows_here, lines_here, triple = block.shape
    model_width = triple // 3
    head_dim = model_width // HEADS
    query_part = block[:, :, :model_width].reshape(rows_here, lines_here, HEADS, head_dim).astype(jnp.float32)
    key_part = block[:, :, model_width:2 * model_width].reshape(rows_here, lines_here, HEADS, head_dim).astype(jnp.float32)
    value_part = block[:, :, 2 * model_width:].reshape(rows_here, lines_here, HEADS, head_dim).astype(jnp.float32)
    scores = jnp.einsum('rnhd,snhd->nhrs', query_part, key_part) / math.sqrt(head_dim)
    weights = jax.nn.softmax(scores, axis=-1).astype(jnp.bfloat16)
    blended = jnp.einsum('nhrs,snhd->rnhd', weights.astype(jnp.float32), value_part)
    return blended.astype(jnp.bfloat16).reshape(rows_here, lines_here, model_width)

def fold_last(patches):
    tokens_here = patches.shape[-2]
    leading = patches.shape[:-2]
    thirds = patches.reshape(leading + (tokens_here, 3, 4))
    blank = jnp.zeros(leading + (tokens_here, 1, 4), patches.dtype)
    summed = jnp.zeros(leading + (2 * tokens_here + 2, 4), patches.dtype)
    for offset in range(3):
        spaced = jnp.concatenate([thirds[..., offset:offset + 1, :], blank], axis=-2)
        spaced = spaced.reshape(leading + (2 * tokens_here, 4))
        padding = [(0, 0)] * len(leading) + [(offset, 2 - offset), (0, 0)]
        summed = summed + jnp.pad(spaced, padding)
    return summed.reshape(leading + ((2 * tokens_here + 2) * 4,))[..., :8 * tokens_here + 4]

def fold_three(patches):
    sectioned = fold_last(patches.transpose(0, 1, 3, 5, 6, 2, 4))
    sectioned = fold_last(sectioned.transpose(1, 2, 4, 5, 0, 3))
    return fold_last(sectioned.transpose(1, 3, 4, 0, 2))

def reference(tokens, ln_gain, w_qkv, w_out, w_rec, solid_top):
    normed = layer_norm(tokens, ln_gain)
    projected_all = jnp.dot(normed.reshape(-1, D), w_qkv, preferred_element_type=jnp.float32).astype(jnp.bfloat16)
    projected_all = projected_all.reshape(ROWS, AISLE, HEIGHT, 3 * D).transpose(1, 0, 2, 3)
    attended = lax.map(attend, projected_all)
    attended = attended.transpose(1, 0, 2, 3).reshape(-1, D)
    branch = jnp.dot(attended, w_out, preferred_element_type=jnp.float32)
    block_out = (tokens.reshape(-1, D).astype(jnp.float32) + branch).astype(jnp.bfloat16)
    block_out = block_out.reshape(ROWS, AISLE, HEIGHT, D)

    def add_block(step, canvas):
        start_token = (jnp.asarray(step) * AD).astype(jnp.int32)
        tile = lax.dynamic_slice_in_dim(block_out, start_token, AD, 1)
        patches = jnp.dot(tile.reshape(-1, D), w_rec, preferred_element_type=jnp.float32)
        patches = patches.reshape(ROWS, AD, HEIGHT, CHANNELS, 12, 12, 12)
        folded = fold_three(patches)[:, 2:-2]
        anchor = jnp.zeros((), jnp.int32)
        corner = (anchor, anchor, anchor, (jnp.asarray(step) * 8 * AD).astype(jnp.int32))
        current = lax.dynamic_slice(canvas, corner, folded.shape)
        return lax.dynamic_update_slice(canvas, current + folded, corner)
    canvas = lax.fori_loop(0, N_AISLE, add_block, jnp.zeros((CHANNELS, ZC, XC + 4, YC + 4), jnp.float32))
    cells = canvas[:, :, 2:-2, 2:-2]
    levels = lax.broadcasted_iota(jnp.int32, (ZC, 1, 1), 0)
    inside_rack = levels < solid_top[None, :, :]
    return jnp.where(inside_rack[None], 0.0, cells).astype(jnp.bfloat16)
```

```python
import jax
import jax.numpy as jnp
from jax import lax
from jax.experimental import pallas as pl
from jax.experimental.pallas import tpu as pltpu
from jax.sharding import PartitionSpec as P

EPSILON = 1e-05
N_ROW, N_AISLE = 32, 8
D, HEADS, DH = 512, 8, 64
MESH = pl.DeviceIdType.MESH
F32, BF16, I32 = jnp.float32, jnp.bfloat16, jnp.int32


def iota(shape, dim):
    return lax.broadcasted_iota(I32, shape, dim)


def one_hot(hit):
    return jnp.where(hit, 1.0, 0.0).astype(BF16)


def dot(a, b):
    return lax.dot_general(a, b, (((1,), (0,)), ((), ())), preferred_element_type=F32)


def dot_nt(a, b):
    return lax.dot_general(a, b, (((1,), (1,)), ((), ())), preferred_element_type=F32)


def send_selector():
    row = iota((256, 1), 0)
    source = (row & 3) * 64 + (row >> 3) * 2 + ((row >> 2) & 1)
    source = jnp.where((row & 3) < 3, source, -1)
    return one_hot(iota((256, 192), 1) == source)


def weight_selector(step):
    row = iota((192, 1), 0)
    main = ((row & 7) + 2) * 12 + (row >> 3) + 2
    below = ((row & 7) + 2) * 12 + ((row >> 3) & 1) + 10
    above = ((row & 7) + 2) * 12 + ((row >> 3) & 1)
    edge = row - 96
    side = jnp.where(edge >= 48, 1, 0)
    edge = edge - 48 * side
    part = edge >> 4
    y = (edge >> 1) & 7
    x = edge & 1
    kx = jnp.where(side == 0, x + 10, x)
    ky = jnp.where(
        part == 0,
        y + 2,
        jnp.where(
            part == 1, jnp.where(y < 2, y + 10, -999), jnp.where(y >= 6, y - 6, -999)
        ),
    )
    edged = kx * 12 + ky
    column = jnp.where(row < 64, main, jnp.where(row < 80, below, jnp.where(row < 96, above, edged)))
    return one_hot(iota((192, 256), 1) - 16 * step == column)


def halo_selector(da, row_index, aisle_index):
    q = iota((384, 1), 0)
    h = jnp.where(q >= 288, 3, jnp.where(q >= 192, 2, jnp.where(q >= 96, 1, 0)))
    rest = q - 96 * h
    r = (rest >> 4) - 1
    a = (rest & 15) + da
    inside = jnp.where(
        r < 0, 256 + a * 4 + h, jnp.where(r > 2, 320 + a * 4 + h, a * 16 + h * 4 + r)
    )
    left = jnp.where(r < 0, 416 + h * 4 + 2, jnp.where(r > 2, 448 + h * 4, 384 + h * 4 + r))
    right = jnp.where(r < 0, 432 + h * 4 + 2, jnp.where(r > 2, 464 + h * 4, 400 + h * 4 + r))
    source = jnp.where(a < 0, left, jnp.where(a > 15, right, inside))
    absent = (
        (r > 3)
        | ((r < 0) & (row_index == 0))
        | ((r > 2) & (row_index == N_ROW - 1))
        | ((a < 0) & (aisle_index == 0))
        | ((a > 15) & (aisle_index == N_AISLE - 1))
    )
    source = jnp.where(absent, -1, source)
    return one_hot(iota((384, 512), 1) == source)


def lane_permutation():
    row = iota((1024, 1), 0)
    r = (row >> 4) & 3
    target = ((row >> 6) & 1) * 384 + r * 128 + (row & 15) * 8 + (row >> 7)
    target = jnp.where(r < 3, target, -1)
    return one_hot(iota((1024, 768), 1) == target)


def edge_selector():
    column = iota((1, 256), 1)
    target = (
        ((column >> 1) & 7) * 64 + (column >> 5) * 8 + ((column >> 4) & 1) * 6 + (column & 1)
    )
    return one_hot(iota((512, 256), 0) == target)


def row_halo_selector():
    row = iota((128, 1), 0)
    source = (row & 63) * 4 + jnp.where(row >= 64, 2, 0)
    return one_hot(iota((128, 256), 1) == source)


def attend_lines(x, gain, w_qkv, w_out):
    center = x - jnp.mean(x, axis=-1, keepdims=True)
    spread = jnp.mean(center * center, axis=-1, keepdims=True)
    normed = (center * lax.rsqrt(spread + EPSILON) * gain).astype(BF16)
    qkv = dot(normed, w_qkv).astype(BF16)
    rows, cols = iota((256, 256), 0), iota((256, 256), 1)
    valid = (((rows ^ cols) & 4) == 0) & ((cols & 3) < 3)
    first = iota((256, 128), 1) < DH
    mask_first = one_hot(first)
    mask_second = 1 - mask_first
    parts = []
    for pair in range(HEADS // 2):
        at = pair * 2 * DH
        query = qkv[:, at : at + 2 * DH]
        key = qkv[:, D + at : D + at + 2 * DH]
        value = qkv[:, 2 * D + at : 2 * D + at + 2 * DH]
        halves = []
        for mask in (mask_first, mask_second):
            scores = dot_nt(query * mask, key) * (1.0 / 8.0)
            scores = jnp.where(valid, scores, -jnp.inf)
            grown = jnp.exp(scores - jnp.max(scores, axis=-1, keepdims=True))
            weights = grown / jnp.sum(grown, axis=-1, keepdims=True)
            halves.append(dot(weights.astype(BF16), value))
        parts.append(jnp.where(first, halves[0], halves[1]).astype(BF16))
    attended = jnp.concatenate(parts, axis=1)
    return x + dot(attended, w_out)


def kernel(
    tokens_ref, gain_ref, w_qkv_hbm, w_out_hbm, w_rec_hbm, solid_ref,
    out_ref,
    w_qkv, w_out, w_rec, send1, recv1, send2, cat, row_halo,
    w_sel, main_w, side_w, edge_w, halo_sel, perm, edge_sel, row_sel,
    shifted, acc, edge_acc, ready,
    load_sem, send_sem, recv_sem,
):
    i, k = lax.axis_index("row"), lax.axis_index("aisle")

    loads = [pltpu.make_async_copy(w_qkv_hbm, w_qkv, load_sem.at[6]),
             pltpu.make_async_copy(w_out_hbm, w_out, load_sem.at[7])]
    for load in loads:
        load.start()

    def rec_load(q):
        columns = pl.ds(pl.multiple_of(q * 1152, 1152), 1152)
        return pltpu.make_async_copy(w_rec_hbm.at[:, columns], w_rec.at[:, columns], load_sem.at[q])

    for q in range(6):
        rec_load(q).start()

    barrier = pltpu.get_barrier_semaphore()

    @pl.loop(1, N_ROW)
    def _(step):
        pl.semaphore_signal(barrier, inc=1, device_id=(lax.rem(i + step, N_ROW), k), device_id_type=MESH)

    up, down = lax.rem(i + 1, N_ROW), lax.rem(i + N_ROW - 1, N_ROW)
    right, left = lax.rem(k + 1, N_AISLE), lax.rem(k + N_AISLE - 1, N_AISLE)
    for device in ((i, right), (i, left), (up, right), (up, left), (down, right), (down, left)):
        pl.semaphore_signal(barrier, inc=1, device_id=device, device_id_type=MESH)

    send1[...] = dot(send_selector(), tokens_ref[...]).reshape(32, 8, D).astype(BF16)
    recv1[i] = send1[i]
    pl.semaphore_wait(barrier, N_ROW - 1 + 6)

    def exchange(source, target, sem):
        @pl.loop(1, N_ROW)
        def _(step):
            j = lax.rem(i + step, N_ROW)
            pltpu.make_async_remote_copy(
                src_ref=source.at[j], dst_ref=target.at[i],
                send_sem=send_sem.at[sem], recv_sem=recv_sem.at[sem],
                device_id=(j, k), device_id_type=MESH,
            ).start()

    def drain(source, target, count, sem, start=0):
        return pltpu.make_async_remote_copy(
            src_ref=source.at[pl.ds(start, count)], dst_ref=target.at[pl.ds(start, count)],
            send_sem=send_sem.at[sem], recv_sem=recv_sem.at[sem],
            device_id=(up, k), device_id_type=MESH,
        )

    exchange(send1, recv1, 0)

    @pl.loop(0, 8)
    def _(s):
        w_sel[s] = weight_selector(s)

    def prepare(q):
        rec_load(q).wait()
        for p in range(4):
            index = q * 4 + p
            c, pair = index // 6, index % 6
            found = []
            for s in (2 * p, 2 * p + 1):
                window = w_rec[:, pl.ds(pl.multiple_of(128 * (9 * q + s), 128), 256)]
                found.append(dot_nt(w_sel[s], window))
            main = [f[:64].reshape(8, 8, D) for f in found]
            main_w[c, :, pair] = jnp.concatenate(main, axis=1).astype(BF16)
            for side in range(2):
                at = 64 + 16 * side
                halves = [f[at : at + 16].reshape(2, 8, D) for f in found]
                side_w[side, c, :, pair] = jnp.concatenate(halves, axis=1).astype(BF16)
                for n in range(2):
                    for part in range(3):
                        at = 96 + 48 * side + 16 * part
                        edge_w[side, c, 2 * pair + n, :, part * D : (part + 1) * D] = found[n][at : at + 16].astype(BF16)

    @pl.loop(0, 3)
    def _(q):
        prepare(q)

    for load in loads:
        load.wait()
    drain(send1, recv1, N_ROW - 1, 0).wait_recv()

    x = recv1[...].astype(F32).reshape(256, D)
    block_out = attend_lines(x, gain_ref[...], w_qkv[...], w_out[...])
    send2[...] = block_out.reshape(32, 8, D).astype(BF16)
    cat[i] = send2[i]
    exchange(send2, cat, 1)

    row_sel[...] = row_halo_selector()
    perm[...] = lane_permutation()
    edge_sel[...] = edge_selector()
    for n, da in enumerate((0, -1, 1)):
        halo_sel[n] = halo_selector(da, i, k)
    shifted[0] = jnp.zeros(shifted.shape[1:], BF16)
    shifted[5] = jnp.zeros(shifted.shape[1:], BF16)
    cat[60:64] = jnp.zeros((4, 8, D), BF16)

    @pl.loop(3, 6)
    def _(q):
        prepare(q)

    drain(send1, recv1, N_ROW - 1, 0).wait_send()
    drain(send2, cat, N_ROW - 1, 1).wait_recv()

    own = cat[:32].astype(F32).reshape(256, D).astype(BF16)
    row_halo[...] = dot(row_sel[...], own).reshape(16, 8, D).astype(BF16)

    def halo_copy(source, at, size, device):
        pltpu.make_async_remote_copy(
            src_ref=source, dst_ref=cat.at[pl.ds(at, size)],
            send_sem=send_sem.at[2], recv_sem=recv_sem.at[2],
            device_id=device, device_id_type=MESH,
        ).start()

    lowest, highest = cat.at[pl.ds(0, 2)], cat.at[pl.ds(30, 2)]
    halo_copy(row_halo.at[pl.ds(0, 8)], 40, 8, (down, k))
    halo_copy(row_halo.at[pl.ds(8, 8)], 32, 8, (up, k))
    halo_copy(lowest, 50, 2, (i, left))
    halo_copy(highest, 48, 2, (i, right))
    halo_copy(highest, 52, 2, (up, right))
    halo_copy(lowest, 54, 2, (up, left))
    halo_copy(highest, 56, 2, (down, right))
    halo_copy(lowest, 58, 2, (down, left))
    drain(send2, cat, N_ROW - 1, 1).wait_send()
    drain(cat, cat, 28, 2, 32).wait_recv()
    drain(cat, cat, 28, 2, 32).wait_send()

    gathered = cat[...].astype(F32).reshape(512, D).astype(BF16)
    for n in range(3):
        picked = dot(halo_sel[n], gathered).reshape(4, 6, 16, D).astype(BF16)
        shifted[1:5, :, :, n * D : (n + 1) * D] = picked

    spans = ((0, 0, 8, 2), (-1, 0, 2, 10), (1, 6, 2, 0))

    @pl.loop(0, 4)
    def _(c):
        for dz, z, n, kz in spans:
            pairs = pl.ds(kz // 2, n // 2)
            here = pl.ds(1 + dz, 4)
            level = pl.ds(z, n)
            for part in range(3):
                token_part = shifted[here, 1:5, :, part * D : (part + 1) * D].reshape(256, D)
                if part == 0:
                    rows, size, y = main_w[c, :, pairs], 8, 0
                else:
                    rows, size, y = side_w[part - 1, c, :, pairs], 2, 6 * (part - 1)
                found = dot_nt(rows.reshape(-1, D), token_part).reshape(size, n, 8, 256)
                if dz == 0 and part == 0:
                    acc[c] = found
                else:
                    acc[c, pl.ds(y, size), level] += found
            for side in range(2):
                token_part = shifted[here, pl.ds(2 * side, 4)].reshape(256, 3 * D)
                rows = edge_w[side, c, pl.ds(kz, n)].reshape(-1, 3 * D)
                found = dot_nt(rows, token_part).reshape(n, 16, 256)
                if dz == 0:
                    edge_acc[c, :, side] = found
                else:
                    edge_acc[c, level, side] += found
        edges = edge_acc[c].reshape(256, 256).astype(BF16)
        total = acc[c].reshape(512, 256) + dot(edge_sel[...], edges)
        total = total.astype(BF16)
        for y in range(8):
            for b in range(2):
                ready[b, c, :, y * 128 : (y + 1) * 128] = total[y * 64 : (y + 1) * 64, b * 128 : (b + 1) * 128]

    solid = solid_ref[...]
    for h in range(4):
        b, low = h // 2, h % 2
        cells = dot(ready[b].reshape(256, 1024), perm[:, low * 384 : (low + 1) * 384])
        cells = jnp.concatenate(
            [cells[:, r * 128 : (r + 1) * 128].reshape(4, 8, 8, 128) for r in range(3)], axis=2
        )
        level = iota((4, 8, 24, 128), 1) + 8 * h
        out_ref[:, 8 * h : 8 * h + 8] = jnp.where(level < solid[None, None], 0.0, cells).astype(BF16)


def body(tokens, ln_gain, w_qkv, w_out, w_rec, solid_top):
    vmem = pl.BlockSpec(memory_space=pltpu.VMEM)
    hbm = pl.BlockSpec(memory_space=pl.ANY)
    return pl.pallas_call(
        kernel,
        out_shape=jax.ShapeDtypeStruct((4, 32, 24, 128), BF16),
        in_specs=[vmem, vmem, hbm, hbm, hbm, vmem],
        out_specs=vmem,
        scratch_shapes=[
            pltpu.VMEM((D, 3 * D), BF16),
            pltpu.VMEM((D, D), BF16),
            pltpu.VMEM((D, 6912), BF16),
            pltpu.VMEM((32, 8, D), BF16),
            pltpu.VMEM((32, 8, D), BF16),
            pltpu.VMEM((32, 8, D), BF16),
            pltpu.VMEM((64, 8, D), BF16),
            pltpu.VMEM((16, 8, D), BF16),
            pltpu.VMEM((8, 192, 256), BF16),
            pltpu.VMEM((4, 8, 6, 16, D), BF16),
            pltpu.VMEM((2, 4, 2, 6, 16, D), BF16),
            pltpu.VMEM((2, 4, 12, 16, 3 * D), BF16),
            pltpu.VMEM((3, 384, 512), BF16),
            pltpu.VMEM((1024, 768), BF16),
            pltpu.VMEM((512, 256), BF16),
            pltpu.VMEM((128, 256), BF16),
            pltpu.VMEM((6, 6, 16, 3 * D), BF16),
            pltpu.VMEM((4, 8, 8, 8, 256), F32),
            pltpu.VMEM((4, 8, 2, 16, 256), F32),
            pltpu.VMEM((2, 4, 64, 1024), BF16),
            pltpu.SemaphoreType.DMA((8,)),
            pltpu.SemaphoreType.DMA((3,)),
            pltpu.SemaphoreType.DMA((3,)),
        ],
        compiler_params=pltpu.CompilerParams(
            collective_id=0, has_side_effects=True, vmem_limit_bytes=52 * 1024 * 1024
        ),
        cost_estimate=pl.CostEstimate(flops=6 * 10**9, bytes_accessed=11 * 10**6, transcendentals=2**19),
        name="airflow_block",
    )(tokens.reshape(192, D), ln_gain.reshape(1, D), w_qkv, w_out, w_rec, solid_top)


def solution(mesh):
    in_specs = (P("row", "aisle", None, None), P(), P(), P(), P(), P("row", "aisle"))
    out_specs = P(None, None, "row", "aisle")
    return jax.shard_map(body, mesh=mesh, in_specs=in_specs, out_specs=out_specs, check_vma=False)
```

```python
import jax
import jax.numpy as jnp
from jax import lax
from jax.experimental import pallas as pl
from jax.experimental.pallas import tpu as pltpu
from jax.sharding import PartitionSpec as P

EPSILON = 1e-05
N_ROW, N_AISLE = 32, 8
D, HEADS, DH = 512, 8, 64
MESH = pl.DeviceIdType.MESH
F32, BF16, I32 = jnp.float32, jnp.bfloat16, jnp.int32


def iota(shape, dim):
    return lax.broadcasted_iota(I32, shape, dim)


def one_hot(hit):
    return jnp.where(hit, 1.0, 0.0).astype(BF16)


def dot(a, b):
    return lax.dot_general(a, b, (((1,), (0,)), ((), ())), preferred_element_type=F32)


def dot_nt(a, b):
    return lax.dot_general(a, b, (((1,), (1,)), ((), ())), preferred_element_type=F32)


def send_selector():
    row = iota((256, 1), 0)
    source = (row & 3) * 64 + (row >> 3) * 2 + ((row >> 2) & 1)
    source = jnp.where((row & 3) < 3, source, -1)
    return one_hot(iota((256, 192), 1) == source)


def weight_selector(step):
    row = iota((192, 1), 0)
    main = ((row & 7) + 2) * 12 + (row >> 3) + 2
    below = ((row & 7) + 2) * 12 + ((row >> 3) & 1) + 10
    above = ((row & 7) + 2) * 12 + ((row >> 3) & 1)
    edge = row - 96
    side = jnp.where(edge >= 48, 1, 0)
    edge = edge - 48 * side
    part = edge >> 4
    y = (edge >> 1) & 7
    x = edge & 1
    kx = jnp.where(side == 0, x + 10, x)
    ky = jnp.where(
        part == 0,
        y + 2,
        jnp.where(
            part == 1, jnp.where(y < 2, y + 10, -999), jnp.where(y >= 6, y - 6, -999)
        ),
    )
    edged = kx * 12 + ky
    column = jnp.where(row < 64, main, jnp.where(row < 80, below, jnp.where(row < 96, above, edged)))
    return one_hot(iota((192, 256), 1) - 16 * step == column)


def halo_selector(da, row_index, aisle_index):
    q = iota((384, 1), 0)
    h = jnp.where(q >= 288, 3, jnp.where(q >= 192, 2, jnp.where(q >= 96, 1, 0)))
    rest = q - 96 * h
    r = (rest >> 4) - 1
    a = (rest & 15) + da
    inside = jnp.where(
        r < 0, 256 + a * 4 + h, jnp.where(r > 2, 320 + a * 4 + h, a * 16 + h * 4 + r)
    )
    left = jnp.where(r < 0, 416 + h * 4 + 2, jnp.where(r > 2, 448 + h * 4, 384 + h * 4 + r))
    right = jnp.where(r < 0, 432 + h * 4 + 2, jnp.where(r > 2, 464 + h * 4, 400 + h * 4 + r))
    source = jnp.where(a < 0, left, jnp.where(a > 15, right, inside))
    absent = (
        (r > 3)
        | ((r < 0) & (row_index == 0))
        | ((r > 2) & (row_index == N_ROW - 1))
        | ((a < 0) & (aisle_index == 0))
        | ((a > 15) & (aisle_index == N_AISLE - 1))
    )
    source = jnp.where(absent, -1, source)
    return one_hot(iota((384, 512), 1) == source)


def lane_permutation():
    row = iota((1024, 1), 0)
    r = (row >> 4) & 3
    target = ((row >> 6) & 1) * 384 + r * 128 + (row & 15) * 8 + (row >> 7)
    target = jnp.where(r < 3, target, -1)
    return one_hot(iota((1024, 768), 1) == target)


def edge_selector():
    column = iota((1, 256), 1)
    target = (
        ((column >> 1) & 7) * 64 + (column >> 5) * 8 + ((column >> 4) & 1) * 6 + (column & 1)
    )
    return one_hot(iota((512, 256), 0) == target)


def row_halo_selector():
    row = iota((128, 1), 0)
    source = (row & 63) * 4 + jnp.where(row >= 64, 2, 0)
    return one_hot(iota((128, 256), 1) == source)


def attend_lines(x, gain, w_qkv, w_out):
    center = x - jnp.mean(x, axis=-1, keepdims=True)
    spread = jnp.mean(center * center, axis=-1, keepdims=True)
    normed = (center * lax.rsqrt(spread + EPSILON) * gain).astype(BF16)
    qkv = dot(normed, w_qkv).astype(BF16)
    rows, cols = iota((256, 256), 0), iota((256, 256), 1)
    valid = (((rows ^ cols) & 4) == 0) & ((cols & 3) < 3)
    first = iota((256, 128), 1) < DH
    mask_first = one_hot(first)
    mask_second = 1 - mask_first
    parts = []
    for pair in range(HEADS // 2):
        at = pair * 2 * DH
        query = qkv[:, at : at + 2 * DH]
        key = qkv[:, D + at : D + at + 2 * DH]
        value = qkv[:, 2 * D + at : 2 * D + at + 2 * DH]
        halves = []
        for mask in (mask_first, mask_second):
            scores = dot_nt(query * mask, key) * (1.0 / 8.0)
            scores = jnp.where(valid, scores, -jnp.inf)
            grown = jnp.exp(scores - jnp.max(scores, axis=-1, keepdims=True))
            weights = grown / jnp.sum(grown, axis=-1, keepdims=True)
            halves.append(dot(weights.astype(BF16), value))
        parts.append(jnp.where(first, halves[0], halves[1]).astype(BF16))
    attended = jnp.concatenate(parts, axis=1)
    return x + dot(attended, w_out)


def kernel(
    tokens_hbm, gain_hbm, w_qkv_hbm, w_out_hbm, w_rec_hbm, solid_hbm,
    out_ref,
    tokens, gain, solid_ref, w_qkv, w_out, w_rec, send1, recv1, send2, cat, row_halo,
    w_sel, main_w, side_w, edge_w, halo_sel, perm, edge_sel, row_sel,
    shifted, acc, edge_acc, ready,
    load_sem, send_sem, recv_sem, halo_send_sem, halo_recv_sem,
):
    i, k = lax.axis_index("row"), lax.axis_index("aisle")

    token_load = pltpu.make_async_copy(tokens_hbm, tokens, load_sem.at[6])
    token_load.start()
    loads = [
        pltpu.make_async_copy(gain_hbm, gain, load_sem.at[7]),
        pltpu.make_async_copy(w_qkv_hbm, w_qkv, load_sem.at[8]),
        pltpu.make_async_copy(w_out_hbm, w_out, load_sem.at[9]),
        pltpu.make_async_copy(solid_hbm, solid_ref, load_sem.at[10]),
    ]
    for load in loads:
        load.start()

    def rec_load(q):
        columns = pl.ds(pl.multiple_of(q * 1152, 1152), 1152)
        return pltpu.make_async_copy(w_rec_hbm.at[:, columns], w_rec.at[:, columns], load_sem.at[q])

    for q in range(6):
        rec_load(q).start()

    barrier = pltpu.get_barrier_semaphore()
    up, down, right, left = i + 1, i - 1, k + 1, k - 1
    has_up, has_down, has_right, has_left = i < N_ROW - 1, i > 0, k < N_AISLE - 1, k > 0
    neighbours = [
        ((i, right), has_right), ((i, left), has_left),
        ((up, right), has_up & has_right), ((up, left), has_up & has_left),
        ((down, right), has_down & has_right), ((down, left), has_down & has_left),
    ]

    @pl.loop(1, N_ROW)
    def _(step):
        pl.semaphore_signal(barrier, inc=1, device_id=(lax.rem(i + step, N_ROW), k), device_id_type=MESH)

    for device, present in neighbours:
        @pl.when(present)
        def _():
            pl.semaphore_signal(barrier, inc=1, device_id=device, device_id_type=MESH)

    token_load.wait()
    mine = tokens[...].astype(F32).reshape(192, D).astype(BF16)
    send1[...] = dot(send_selector(), mine).reshape(32, 8, D).astype(BF16)
    recv1[i] = send1[i]
    across = has_left.astype(I32) + has_right.astype(I32)
    along = has_down.astype(I32) + has_up.astype(I32)
    pl.semaphore_wait(barrier, N_ROW - 1 + across * (1 + along))

    def exchange(source, target, sem):
        @pl.loop(1, N_ROW)
        def _(step):
            j = lax.rem(i + step, N_ROW)
            pltpu.make_async_remote_copy(
                src_ref=source.at[j], dst_ref=target.at[i],
                send_sem=send_sem.at[sem], recv_sem=recv_sem.at[sem],
                device_id=(j, k), device_id_type=MESH,
            ).start()

    def drain(source, target, count, sem, start=0):
        return pltpu.make_async_remote_copy(
            src_ref=source.at[pl.ds(start, count)], dst_ref=target.at[pl.ds(start, count)],
            send_sem=send_sem.at[sem], recv_sem=recv_sem.at[sem],
            device_id=(lax.rem(i + 1, N_ROW), k), device_id_type=MESH,
        )

    exchange(send1, recv1, 0)

    @pl.loop(0, 8)
    def _(s):
        w_sel[s] = weight_selector(s)

    def prepare(q):
        rec_load(q).wait()
        for p in range(4):
            index = q * 4 + p
            c, pair = index // 6, index % 6
            found = []
            for s in (2 * p, 2 * p + 1):
                window = w_rec[:, pl.ds(pl.multiple_of(128 * (9 * q + s), 128), 256)]
                found.append(dot_nt(w_sel[s], window))
            main = [f[:64].reshape(8, 8, D) for f in found]
            main_w[c, :, pair] = jnp.concatenate(main, axis=1).astype(BF16)
            for side in range(2):
                at = 64 + 16 * side
                halves = [f[at : at + 16].reshape(2, 8, D) for f in found]
                side_w[side, c, :, pair] = jnp.concatenate(halves, axis=1).astype(BF16)
                for n in range(2):
                    for part in range(3):
                        at = 96 + 48 * side + 16 * part
                        edge_w[side, c, 2 * pair + n, :, part * D : (part + 1) * D] = found[n][at : at + 16].astype(BF16)

    @pl.loop(0, 3)
    def _(q):
        prepare(q)

    for load in loads:
        load.wait()
    drain(send1, recv1, N_ROW - 1, 0).wait_recv()

    x = recv1[...].astype(F32).reshape(256, D)
    block_out = attend_lines(x, gain[...], w_qkv[...], w_out[...])
    send2[...] = block_out.reshape(32, 8, D).astype(BF16)
    cat[i] = send2[i]
    exchange(send2, cat, 1)

    row_sel[...] = row_halo_selector()
    perm[...] = lane_permutation()
    edge_sel[...] = edge_selector()
    for n, da in enumerate((0, -1, 1)):
        halo_sel[n] = halo_selector(da, i, k)
    shifted[0] = jnp.zeros(shifted.shape[1:], BF16)
    shifted[5] = jnp.zeros(shifted.shape[1:], BF16)
    for n, size, present in ((32, 8, has_down), (40, 8, has_up)):
        @pl.when(jnp.logical_not(present))
        def _():
            cat[n : n + size] = jnp.zeros((size, 8, D), BF16)
    sides = [has_left, has_right, has_down & has_left, has_down & has_right, has_up & has_left, has_up & has_right]
    for n, present in enumerate(sides):
        @pl.when(jnp.logical_not(present))
        def _():
            cat[48 + 2 * n : 50 + 2 * n] = jnp.zeros((2, 8, D), BF16)
    cat[60:64] = jnp.zeros((4, 8, D), BF16)

    @pl.loop(3, 6)
    def _(q):
        prepare(q)

    drain(send1, recv1, N_ROW - 1, 0).wait_send()
    drain(send2, cat, N_ROW - 1, 1).wait_recv()

    own = cat[:32].astype(F32).reshape(256, D).astype(BF16)
    row_halo[...] = dot(row_sel[...], own).reshape(16, 8, D).astype(BF16)

    lowest, highest = cat.at[pl.ds(0, 2)], cat.at[pl.ds(30, 2)]
    halos = [
        (row_halo.at[pl.ds(0, 8)], 40, (down, k), has_down),
        (row_halo.at[pl.ds(8, 8)], 32, (up, k), has_up),
        (lowest, 50, (i, left), has_left),
        (highest, 48, (i, right), has_right),
        (highest, 52, (up, right), has_up & has_right),
        (lowest, 54, (up, left), has_up & has_left),
        (highest, 56, (down, right), has_down & has_right),
        (lowest, 58, (down, left), has_down & has_left),
    ]

    def halo_copy(n):
        source, at, device, _ = halos[n]
        return pltpu.make_async_remote_copy(
            src_ref=source, dst_ref=cat.at[pl.ds(at, 8 if n < 2 else 2)],
            send_sem=halo_send_sem.at[n], recv_sem=halo_recv_sem.at[n],
            device_id=device, device_id_type=MESH,
        )

    for n in range(8):
        @pl.when(halos[n][3])
        def _():
            halo_copy(n).start()

    drain(send2, cat, N_ROW - 1, 1).wait_send()
    arrives = [has_up, has_down, has_right, has_left, has_down & has_left, has_down & has_right, has_up & has_left, has_up & has_right]
    for n in range(8):
        @pl.when(arrives[n])
        def _():
            halo_copy(n).wait_recv()

        @pl.when(halos[n][3])
        def _():
            halo_copy(n).wait_send()


    gathered = cat[...].astype(F32).reshape(512, D).astype(BF16)
    for n in range(3):
        picked = dot(halo_sel[n], gathered).reshape(4, 6, 16, D).astype(BF16)
        shifted[1:5, :, :, n * D : (n + 1) * D] = picked

    spans = ((0, 0, 8, 2), (-1, 0, 2, 10), (1, 6, 2, 0))

    for dz, z, n, kz in spans:
        pairs = pl.ds(kz // 2, n // 2)
        here = pl.ds(1 + dz, 4)
        level = pl.ds(z, n)
        for part in range(3):
            token_part = shifted[here, 1:5, :, part * D : (part + 1) * D].reshape(256, D)
            if part == 0:
                rows, size, y = main_w[:, :, pairs], 8, 0
            else:
                rows, size, y = side_w[part - 1, :, :, pairs], 2, 6 * (part - 1)
            found = dot_nt(rows.reshape(-1, D), token_part).reshape(4, size, n, 8, 256)
            if dz == 0 and part == 0:
                acc[...] = found
            else:
                acc[:, pl.ds(y, size), level] += found
        for side in range(2):
            token_part = shifted[here, pl.ds(2 * side, 4)].reshape(256, 3 * D)
            rows = edge_w[side, :, pl.ds(kz, n)].reshape(-1, 3 * D)
            found = dot_nt(rows, token_part).reshape(4, n, 16, 256)
            if dz == 0:
                edge_acc[:, :, side] = found
            else:
                edge_acc[:, level, side] += found
    for c in range(4):
        edges = edge_acc[c].reshape(256, 256).astype(BF16)
        total = acc[c].reshape(512, 256) + dot(edge_sel[...], edges)
        total = total.astype(BF16)
        for y in range(8):
            for b in range(2):
                ready[b, c, :, y * 128 : (y + 1) * 128] = total[y * 64 : (y + 1) * 64, b * 128 : (b + 1) * 128]
    solid = solid_ref[...]
    for low in range(2):
        cells = dot(ready[...].reshape(512, 1024), perm[:, low * 384 : (low + 1) * 384])
        for b in range(2):
            h = 2 * b + low
            part = cells[b * 256 : (b + 1) * 256]
            part = jnp.concatenate(
                [part[:, r * 128 : (r + 1) * 128].reshape(4, 8, 8, 128) for r in range(3)], axis=2
            )
            level = iota((4, 8, 24, 128), 1) + 8 * h
            out_ref[:, 8 * h : 8 * h + 8] = jnp.where(level < solid[None, None], 0.0, part).astype(BF16)


def body(tokens, ln_gain, w_qkv, w_out, w_rec, solid_top):
    vmem = pl.BlockSpec(memory_space=pltpu.VMEM)
    hbm = pl.BlockSpec(memory_space=pltpu.HBM)
    return pl.pallas_call(
        kernel,
        out_shape=jax.ShapeDtypeStruct((4, 32, 24, 128), BF16),
        in_specs=[hbm] * 6,
        out_specs=vmem,
        scratch_shapes=[
            pltpu.VMEM((3, 16, 4, D), BF16),
            pltpu.VMEM((1, D), F32),
            pltpu.VMEM((24, 128), I32),
            pltpu.VMEM((D, 3 * D), BF16),
            pltpu.VMEM((D, D), BF16),
            pltpu.VMEM((D, 6912), BF16),
            pltpu.VMEM((32, 8, D), BF16),
            pltpu.VMEM((32, 8, D), BF16),
            pltpu.VMEM((32, 8, D), BF16),
            pltpu.VMEM((64, 8, D), BF16),
            pltpu.VMEM((16, 8, D), BF16),
            pltpu.VMEM((8, 192, 256), BF16),
            pltpu.VMEM((4, 8, 6, 16, D), BF16),
            pltpu.VMEM((2, 4, 2, 6, 16, D), BF16),
            pltpu.VMEM((2, 4, 12, 16, 3 * D), BF16),
            pltpu.VMEM((3, 384, 512), BF16),
            pltpu.VMEM((1024, 768), BF16),
            pltpu.VMEM((512, 256), BF16),
            pltpu.VMEM((128, 256), BF16),
            pltpu.VMEM((6, 6, 16, 3 * D), BF16),
            pltpu.VMEM((4, 8, 8, 8, 256), F32),
            pltpu.VMEM((4, 8, 2, 16, 256), F32),
            pltpu.VMEM((2, 4, 64, 1024), BF16),
            pltpu.SemaphoreType.DMA((11,)),
            pltpu.SemaphoreType.DMA((2,)),
            pltpu.SemaphoreType.DMA((2,)),
            pltpu.SemaphoreType.DMA((8,)),
            pltpu.SemaphoreType.DMA((8,)),
        ],
        compiler_params=pltpu.CompilerParams(
            collective_id=0, has_side_effects=True, vmem_limit_bytes=60 * 1024 * 1024
        ),
        cost_estimate=pl.CostEstimate(flops=6 * 10**9, bytes_accessed=11 * 10**6, transcendentals=2**19),
        name="airflow_block",
    )(tokens, ln_gain.reshape(1, D), w_qkv, w_out, w_rec, solid_top)


def solution(mesh):
    in_specs = (P("row", "aisle", None, None), P(), P(), P(), P(), P("row", "aisle"))
    out_specs = P(None, None, "row", "aisle")
    return jax.shard_map(body, mesh=mesh, in_specs=in_specs, out_specs=out_specs, check_vma=False)
```

```python
import jax
import jax.numpy as jnp
from jax import lax
from jax.experimental import pallas as pl
from jax.experimental.pallas import tpu as pltpu
from jax.sharding import PartitionSpec as P

EPSILON = 1e-05
N_ROW, N_AISLE = 32, 8
D, HEADS, DH = 512, 8, 64
MESH = pl.DeviceIdType.MESH
F32, BF16, I32 = jnp.float32, jnp.bfloat16, jnp.int32


def iota(shape, dim):
    return lax.broadcasted_iota(I32, shape, dim)


def one_hot(hit):
    return jnp.where(hit, 1.0, 0.0).astype(BF16)


def dot(a, b):
    return lax.dot_general(a, b, (((1,), (0,)), ((), ())), preferred_element_type=F32)


def dot_nt(a, b):
    return lax.dot_general(a, b, (((1,), (1,)), ((), ())), preferred_element_type=F32)


def send_selector():
    row = iota((256, 1), 0)
    source = (row & 3) * 64 + (row >> 3) * 2 + ((row >> 2) & 1)
    source = jnp.where((row & 3) < 3, source, -1)
    return one_hot(iota((256, 192), 1) == source)


def weight_selector(step):
    row = iota((192, 1), 0)
    main = ((row & 7) + 2) * 12 + (row >> 3) + 2
    below = ((row & 7) + 2) * 12 + ((row >> 3) & 1) + 10
    above = ((row & 7) + 2) * 12 + ((row >> 3) & 1)
    edge = row - 96
    side = jnp.where(edge >= 48, 1, 0)
    edge = edge - 48 * side
    part = edge >> 4
    y = (edge >> 1) & 7
    x = edge & 1
    kx = jnp.where(side == 0, x + 10, x)
    ky = jnp.where(
        part == 0,
        y + 2,
        jnp.where(
            part == 1, jnp.where(y < 2, y + 10, -999), jnp.where(y >= 6, y - 6, -999)
        ),
    )
    edged = kx * 12 + ky
    column = jnp.where(row < 64, main, jnp.where(row < 80, below, jnp.where(row < 96, above, edged)))
    return one_hot(iota((192, 256), 1) - 16 * step == column)


def halo_selector(da, row_index, aisle_index):
    q = iota((384, 1), 0)
    h = jnp.where(q >= 288, 3, jnp.where(q >= 192, 2, jnp.where(q >= 96, 1, 0)))
    rest = q - 96 * h
    r = (rest >> 4) - 1
    a = (rest & 15) + da
    inside = jnp.where(
        r < 0, 256 + a * 4 + h, jnp.where(r > 2, 320 + a * 4 + h, a * 16 + h * 4 + r)
    )
    left = jnp.where(r < 0, 416 + h, jnp.where(r > 2, 432 + h, 384 + h * 4 + r))
    right = jnp.where(r < 0, 424 + h, jnp.where(r > 2, 440 + h, 400 + h * 4 + r))
    source = jnp.where(a < 0, left, jnp.where(a > 15, right, inside))
    absent = (
        (r > 3)
        | ((r < 0) & (row_index == 0))
        | ((r > 2) & (row_index == N_ROW - 1))
        | ((a < 0) & (aisle_index == 0))
        | ((a > 15) & (aisle_index == N_AISLE - 1))
    )
    source = jnp.where(absent, -1, source)
    return one_hot(iota((384, 512), 1) == source)


def lane_permutation():
    row = iota((1024, 1), 0)
    r = (row >> 4) & 3
    target = ((row >> 6) & 1) * 384 + r * 128 + (row & 15) * 8 + (row >> 7)
    target = jnp.where(r < 3, target, -1)
    return one_hot(iota((1024, 768), 1) == target)


def edge_selector():
    column = iota((1, 256), 1)
    target = (
        ((column >> 1) & 7) * 64 + (column >> 5) * 8 + ((column >> 4) & 1) * 6 + (column & 1)
    )
    return one_hot(iota((512, 256), 0) == target)


def row_halo_selector():
    row = iota((160, 1), 0)
    edge = (row & 63) * 4 + jnp.where(row >= 64, 2, 0)
    block = (row - 128) >> 3
    corner = (row & 7) * 4 + jnp.where(block < 2, 2, 0) + jnp.where((block & 1) == 0, 240, 0)
    source = jnp.where(row < 128, edge, jnp.where((row & 7) < 4, corner, -1))
    return one_hot(iota((160, 256), 1) == source)


def attend_lines(x, gain, w_qkv, w_out):
    center = x - jnp.mean(x, axis=-1, keepdims=True)
    spread = jnp.mean(center * center, axis=-1, keepdims=True)
    normed = (center * lax.rsqrt(spread + EPSILON) * gain).astype(BF16)
    qkv = dot(normed, w_qkv).astype(BF16)
    rows, cols = iota((256, 256), 0), iota((256, 256), 1)
    valid = (((rows ^ cols) & 4) == 0) & ((cols & 3) < 3)
    first = iota((256, 128), 1) < DH
    mask_first = one_hot(first)
    mask_second = 1 - mask_first
    parts = []
    for pair in range(HEADS // 2):
        at = pair * 2 * DH
        query = qkv[:, at : at + 2 * DH]
        key = qkv[:, D + at : D + at + 2 * DH]
        value = qkv[:, 2 * D + at : 2 * D + at + 2 * DH]
        halves = []
        for mask in (mask_first, mask_second):
            scores = dot_nt(query * mask, key) * (1.0 / 8.0)
            scores = jnp.where(valid, scores, -jnp.inf)
            grown = jnp.exp(scores - jnp.max(scores, axis=-1, keepdims=True))
            weights = grown / jnp.sum(grown, axis=-1, keepdims=True)
            halves.append(dot(weights.astype(BF16), value))
        parts.append(jnp.where(first, halves[0], halves[1]).astype(BF16))
    attended = jnp.concatenate(parts, axis=1)
    return x + dot(attended, w_out)


def kernel(
    tokens_hbm, gain_hbm, w_qkv_hbm, w_out_hbm, w_rec_hbm,
    out_ref,
    tokens, gain, w_qkv, w_out, w_rec, send1, recv1, send2, cat, row_halo,
    w_sel, main_w, side_w, edge_w, halo_sel, perm, edge_sel, row_sel,
    shifted, acc, edge_acc, ready, found_cells,
    load_sem, send_sem, recv_sem, halo_send_sem, halo_recv_sem, store_sem,
):
    i, k = lax.axis_index("row"), lax.axis_index("aisle")

    token_load = pltpu.make_async_copy(tokens_hbm, tokens, load_sem.at[6])
    token_load.start()
    loads = [
        pltpu.make_async_copy(gain_hbm, gain, load_sem.at[7]),
        pltpu.make_async_copy(w_qkv_hbm, w_qkv, load_sem.at[8]),
        pltpu.make_async_copy(w_out_hbm, w_out, load_sem.at[9]),
    ]
    for load in loads:
        load.start()

    def rec_load(q):
        columns = pl.ds(pl.multiple_of(q * 1152, 1152), 1152)
        return pltpu.make_async_copy(w_rec_hbm.at[:, columns], w_rec.at[:, columns], load_sem.at[q])

    for q in range(6):
        rec_load(q).start()

    barrier = pltpu.get_barrier_semaphore()
    up, down, right, left = i + 1, i - 1, k + 1, k - 1
    has_up, has_down, has_right, has_left = i < N_ROW - 1, i > 0, k < N_AISLE - 1, k > 0
    neighbours = [
        ((i, right), has_right), ((i, left), has_left),
        ((up, right), has_up & has_right), ((up, left), has_up & has_left),
        ((down, right), has_down & has_right), ((down, left), has_down & has_left),
    ]

    @pl.loop(1, N_ROW)
    def _(step):
        pl.semaphore_signal(barrier, inc=1, device_id=(lax.rem(i + step, N_ROW), k), device_id_type=MESH)

    for device, present in neighbours:
        @pl.when(present)
        def _():
            pl.semaphore_signal(barrier, inc=1, device_id=device, device_id_type=MESH)

    token_load.wait()
    mine = tokens[...].astype(F32).reshape(192, D).astype(BF16)
    send1[...] = dot(send_selector(), mine).reshape(32, 8, D).astype(BF16)
    recv1[i] = send1[i]
    across = has_left.astype(I32) + has_right.astype(I32)
    along = has_down.astype(I32) + has_up.astype(I32)
    pl.semaphore_wait(barrier, N_ROW - 1 + across * (1 + along))

    def exchange(source, target, sem):
        @pl.loop(1, N_ROW)
        def _(step):
            j = lax.rem(i + step, N_ROW)
            pltpu.make_async_remote_copy(
                src_ref=source.at[j], dst_ref=target.at[i],
                send_sem=send_sem.at[sem], recv_sem=recv_sem.at[sem],
                device_id=(j, k), device_id_type=MESH,
            ).start()

    def drain(source, target, count, sem, start=0):
        return pltpu.make_async_remote_copy(
            src_ref=source.at[pl.ds(start, count)], dst_ref=target.at[pl.ds(start, count)],
            send_sem=send_sem.at[sem], recv_sem=recv_sem.at[sem],
            device_id=(lax.rem(i + 1, N_ROW), k), device_id_type=MESH,
        )

    exchange(send1, recv1, 0)

    @pl.loop(0, 8)
    def _(s):
        w_sel[s] = weight_selector(s)

    def prepare(q):
        rec_load(q).wait()
        for p in range(4):
            index = q * 4 + p
            c, pair = index // 6, index % 6
            found = []
            for s in (2 * p, 2 * p + 1):
                window = w_rec[:, pl.ds(pl.multiple_of(128 * (9 * q + s), 128), 256)]
                found.append(dot_nt(w_sel[s], window))
            main = [f[:64].reshape(8, 8, D) for f in found]
            main_w[c, :, pair] = jnp.concatenate(main, axis=1).astype(BF16)
            for side in range(2):
                at = 64 + 16 * side
                halves = [f[at : at + 16].reshape(2, 8, D) for f in found]
                side_w[side, c, :, pair] = jnp.concatenate(halves, axis=1).astype(BF16)
                for n in range(2):
                    for part in range(3):
                        at = 96 + 48 * side + 16 * part
                        edge_w[side, c, 2 * pair + n, :, part * D : (part + 1) * D] = found[n][at : at + 16].astype(BF16)

    @pl.loop(0, 3)
    def _(q):
        prepare(q)

    for load in loads:
        load.wait()
    drain(send1, recv1, N_ROW - 1, 0).wait_recv()

    x = recv1[...].astype(F32).reshape(256, D)
    block_out = attend_lines(x, gain[...], w_qkv[...], w_out[...])
    send2[...] = block_out.reshape(32, 8, D).astype(BF16)
    cat[i] = send2[i]
    exchange(send2, cat, 1)

    row_sel[...] = row_halo_selector()
    perm[...] = lane_permutation()
    edge_sel[...] = edge_selector()
    for n, da in enumerate((0, -1, 1)):
        halo_sel[n] = halo_selector(da, i, k)
    shifted[0] = jnp.zeros(shifted.shape[1:], BF16)
    shifted[5] = jnp.zeros(shifted.shape[1:], BF16)
    for n, size, present in ((32, 8, has_down), (40, 8, has_up)):
        @pl.when(jnp.logical_not(present))
        def _():
            cat[n : n + size] = jnp.zeros((size, 8, D), BF16)
    sides = [has_left, has_right, has_down & has_left, has_down & has_right, has_up & has_left, has_up & has_right]
    for n, present in enumerate(sides):
        @pl.when(jnp.logical_not(present))
        def _():
            at, size = (48 + 2 * n, 2) if n < 2 else (50 + n, 1)
            cat[at : at + size] = jnp.zeros((size, 8, D), BF16)
    cat[56:64] = jnp.zeros((8, 8, D), BF16)

    @pl.loop(3, 6)
    def _(q):
        prepare(q)

    drain(send1, recv1, N_ROW - 1, 0).wait_send()
    drain(send2, cat, N_ROW - 1, 1).wait_recv()

    lowest, highest = cat.at[pl.ds(0, 2)], cat.at[pl.ds(30, 2)]
    halos = [
        (row_halo.at[pl.ds(0, 8)], 40, 8, (down, k), has_down),
        (row_halo.at[pl.ds(8, 8)], 32, 8, (up, k), has_up),
        (lowest, 50, 2, (i, left), has_left),
        (highest, 48, 2, (i, right), has_right),
        (row_halo.at[pl.ds(16, 1)], 52, 1, (up, right), has_up & has_right),
        (row_halo.at[pl.ds(17, 1)], 53, 1, (up, left), has_up & has_left),
        (row_halo.at[pl.ds(18, 1)], 54, 1, (down, right), has_down & has_right),
        (row_halo.at[pl.ds(19, 1)], 55, 1, (down, left), has_down & has_left),
    ]

    def halo_copy(n):
        source, at, size, device, _ = halos[n]
        return pltpu.make_async_remote_copy(
            src_ref=source, dst_ref=cat.at[pl.ds(at, size)],
            send_sem=halo_send_sem.at[n], recv_sem=halo_recv_sem.at[n],
            device_id=device, device_id_type=MESH,
        )

    def start_halos(numbers):
        for n in numbers:
            @pl.when(halos[n][4])
            def _():
                halo_copy(n).start()

    start_halos((2, 3))
    own = cat[:32].astype(F32).reshape(256, D).astype(BF16)
    row_halo[...] = dot(row_sel[...], own).reshape(20, 8, D).astype(BF16)
    start_halos((4, 5, 6, 7, 0, 1))

    shifted[1:5, :, :, :D] = dot(halo_sel[0, :, :256], own).reshape(4, 6, 16, D).astype(BF16)
    spans = ((0, 0, 8, 2), (-1, 0, 2, 10), (1, 6, 2, 0))
    for dz, z, n, kz in spans:
        token_part = shifted[1 + dz : 5 + dz, 1:5, :, :D].reshape(256, D)
        rows = main_w[:, :, kz // 2 : (kz + n) // 2].reshape(-1, D)
        found = dot_nt(rows, token_part).reshape(4, 8, n, 8, 256)
        if dz == 0:
            acc[...] = found
        else:
            acc[:, :, z : z + n] += found

    drain(send2, cat, N_ROW - 1, 1).wait_send()
    arrives = [has_up, has_down, has_right, has_left, has_down & has_left, has_down & has_right, has_up & has_left, has_up & has_right]
    for n in range(8):
        @pl.when(arrives[n])
        def _():
            halo_copy(n).wait_recv()

        @pl.when(halos[n][4])
        def _():
            halo_copy(n).wait_send()


    gathered = cat[...].astype(F32).reshape(512, D).astype(BF16)
    for n in range(3):
        picked = dot(halo_sel[n], gathered).reshape(4, 6, 16, D).astype(BF16)
        shifted[1:5, :, :, n * D : (n + 1) * D] = picked

    spans = ((0, 0, 8, 2), (-1, 0, 2, 10), (1, 6, 2, 0))

    for dz, z, n, kz in spans:
        here = pl.ds(1 + dz, 4)
        level = pl.ds(z, n)
        for side in range(2):
            token_part = shifted[here, 1:5, :, (side + 1) * D : (side + 2) * D].reshape(256, D)
            rows = side_w[side, :, :, pl.ds(kz // 2, n // 2)].reshape(-1, D)
            acc[:, pl.ds(6 * side, 2), level] += dot_nt(rows, token_part).reshape(4, 2, n, 8, 256)
            token_part = shifted[here, pl.ds(2 * side, 4)].reshape(256, 3 * D)
            rows = edge_w[side, :, pl.ds(kz, n)].reshape(-1, 3 * D)
            found = dot_nt(rows, token_part).reshape(4, n, 16, 256)
            if dz == 0:
                edge_acc[:, :, side] = found
            else:
                edge_acc[:, level, side] += found
    for c in range(4):
        edges = edge_acc[c].reshape(256, 256).astype(BF16)
        total = acc[c].reshape(512, 256) + dot(edge_sel[...], edges)
        total = total.astype(BF16)
        for y in range(8):
            for b in range(2):
                ready[b, c, :, y * 128 : (y + 1) * 128] = total[y * 64 : (y + 1) * 64, b * 128 : (b + 1) * 128]
    stores = []
    for low in range(2):
        cells = dot(ready[...].reshape(512, 1024), perm[:, low * 384 : (low + 1) * 384])
        for b in range(2):
            h = 2 * b + low
            for r in range(3):
                part = cells[b * 256 : (b + 1) * 256, r * 128 : (r + 1) * 128]
                found_cells[h, :, :, 8 * r : 8 * r + 8] = part.reshape(4, 8, 8, 128)
            store = pltpu.make_async_copy(
                found_cells.at[h], out_ref.at[:, pl.ds(8 * h, 8)], store_sem.at[h]
            )
            store.start()
            stores.append(store)
    for store in stores:
        store.wait()


def body(tokens, ln_gain, w_qkv, w_out, w_rec, solid_top):
    hbm = pl.BlockSpec(memory_space=pltpu.HBM)
    cells = pl.pallas_call(
        kernel,
        out_shape=jax.ShapeDtypeStruct((4, 32, 24, 128), F32),
        in_specs=[hbm] * 5,
        out_specs=hbm,
        scratch_shapes=[
            pltpu.VMEM((3, 16, 4, D), BF16),
            pltpu.VMEM((1, D), F32),
            pltpu.VMEM((D, 3 * D), BF16),
            pltpu.VMEM((D, D), BF16),
            pltpu.VMEM((D, 6912), BF16),
            pltpu.VMEM((32, 8, D), BF16),
            pltpu.VMEM((32, 8, D), BF16),
            pltpu.VMEM((32, 8, D), BF16),
            pltpu.VMEM((64, 8, D), BF16),
            pltpu.VMEM((20, 8, D), BF16),
            pltpu.VMEM((8, 192, 256), BF16),
            pltpu.VMEM((4, 8, 6, 16, D), BF16),
            pltpu.VMEM((2, 4, 2, 6, 16, D), BF16),
            pltpu.VMEM((2, 4, 12, 16, 3 * D), BF16),
            pltpu.VMEM((3, 384, 512), BF16),
            pltpu.VMEM((1024, 768), BF16),
            pltpu.VMEM((512, 256), BF16),
            pltpu.VMEM((160, 256), BF16),
            pltpu.VMEM((6, 6, 16, 3 * D), BF16),
            pltpu.VMEM((4, 8, 8, 8, 256), F32),
            pltpu.VMEM((4, 8, 2, 16, 256), F32),
            pltpu.VMEM((2, 4, 64, 1024), BF16),
            pltpu.VMEM((4, 4, 8, 24, 128), F32),
            pltpu.SemaphoreType.DMA((10,)),
            pltpu.SemaphoreType.DMA((2,)),
            pltpu.SemaphoreType.DMA((2,)),
            pltpu.SemaphoreType.DMA((8,)),
            pltpu.SemaphoreType.DMA((8,)),
            pltpu.SemaphoreType.DMA((4,)),
        ],
        compiler_params=pltpu.CompilerParams(
            collective_id=0, has_side_effects=True, vmem_limit_bytes=60 * 1024 * 1024
        ),
        cost_estimate=pl.CostEstimate(flops=6 * 10**9, bytes_accessed=11 * 10**6, transcendentals=2**19),
        name="airflow_block",
    )(tokens, ln_gain.reshape(1, D), w_qkv, w_out, w_rec)
    level = iota((4, 32, 24, 128), 1)
    return jnp.where(level < solid_top[None, None], 0.0, cells).astype(BF16)


def solution(mesh):
    in_specs = (P("row", "aisle", None, None), P(), P(), P(), P(), P("row", "aisle"))
    out_specs = P(None, None, "row", "aisle")
    return jax.shard_map(body, mesh=mesh, in_specs=in_specs, out_specs=out_specs, check_vma=False)
```

```python
import jax
import jax.numpy as jnp
from jax import lax
from jax.experimental import pallas as pl
from jax.experimental.pallas import tpu as pltpu
from jax.sharding import PartitionSpec as P

EPSILON = 1e-05
N_ROW, N_AISLE = 32, 8
D, HEADS, DH = 512, 8, 64
MESH = pl.DeviceIdType.MESH
F32, BF16, I32 = jnp.float32, jnp.bfloat16, jnp.int32


def iota(shape, dim):
    return lax.broadcasted_iota(I32, shape, dim)


def one_hot(hit):
    return jnp.where(hit, 1.0, 0.0).astype(BF16)


def dot(a, b):
    return lax.dot_general(a, b, (((1,), (0,)), ((), ())), preferred_element_type=F32)


def dot_nt(a, b):
    return lax.dot_general(a, b, (((1,), (1,)), ((), ())), preferred_element_type=F32)


def send_selector():
    row = iota((256, 1), 0)
    source = (row & 3) * 64 + (row >> 3) * 2 + ((row >> 2) & 1)
    source = jnp.where((row & 3) < 3, source, -1)
    return one_hot(iota((256, 192), 1) == source)


def weight_selector(step):
    row = iota((192, 1), 0)
    main = ((row & 7) + 2) * 12 + (row >> 3) + 2
    below = ((row & 7) + 2) * 12 + ((row >> 3) & 1) + 10
    above = ((row & 7) + 2) * 12 + ((row >> 3) & 1)
    edge = row - 96
    side = jnp.where(edge >= 48, 1, 0)
    edge = edge - 48 * side
    part = edge >> 4
    y = (edge >> 1) & 7
    x = edge & 1
    kx = jnp.where(side == 0, x + 10, x)
    ky = jnp.where(
        part == 0,
        y + 2,
        jnp.where(
            part == 1, jnp.where(y < 2, y + 10, -999), jnp.where(y >= 6, y - 6, -999)
        ),
    )
    edged = kx * 12 + ky
    column = jnp.where(row < 64, main, jnp.where(row < 80, below, jnp.where(row < 96, above, edged)))
    return one_hot(iota((192, 256), 1) - 16 * step == column)


def near_selector(da):
    q = iota((192, 1), 0)
    h = jnp.where(q >= 144, 3, jnp.where(q >= 96, 2, jnp.where(q >= 48, 1, 0)))
    rest = q - 48 * h
    r, a = rest >> 4, (rest & 15) + da
    block = jnp.where(a < 0, 16, jnp.where(a > 15, 17, a))
    return one_hot(iota((192, 384), 1) == block * 16 + h * 4 + r)


def far_selector(da):
    q = iota((128, 1), 0)
    h, side, a = q >> 5, (q >> 4) & 1, (q & 15) + da
    block = jnp.where(a < 0, 16, jnp.where(a > 15, 17, a))
    return one_hot(iota((128, 256), 1) == side * 72 + block * 4 + h)


def lane_permutation():
    row = iota((1024, 1), 0)
    r = (row >> 4) & 3
    target = ((row >> 6) & 1) * 384 + r * 128 + (row & 15) * 8 + (row >> 7)
    target = jnp.where(r < 3, target, -1)
    return one_hot(iota((1024, 768), 1) == target)


def edge_selector():
    column = iota((1, 256), 1)
    target = (
        ((column >> 1) & 7) * 64 + (column >> 5) * 8 + ((column >> 4) & 1) * 6 + (column & 1)
    )
    return one_hot(iota((512, 256), 0) == target)


def row_halo_selector():
    row = iota((144, 1), 0)
    source = jnp.where(row >= 72, (row - 72) * 4 + 2, row * 4)
    return one_hot(iota((144, 384), 1) == source)


def attend_lines(x, gain, w_qkv, w_out):
    center = x - jnp.mean(x, axis=-1, keepdims=True)
    spread = jnp.mean(center * center, axis=-1, keepdims=True)
    normed = (center * lax.rsqrt(spread + EPSILON) * gain).astype(BF16)
    qkv = dot(normed, w_qkv).astype(BF16)
    rows, cols = iota((256, 256), 0), iota((256, 256), 1)
    valid = (((rows ^ cols) & 4) == 0) & ((cols & 3) < 3)
    first = iota((256, 128), 1) < DH
    mask_first = one_hot(first)
    mask_second = 1 - mask_first
    parts = []
    for pair in range(HEADS // 2):
        at = pair * 2 * DH
        query = qkv[:, at : at + 2 * DH]
        key = qkv[:, D + at : D + at + 2 * DH]
        value = qkv[:, 2 * D + at : 2 * D + at + 2 * DH]
        halves = []
        for mask in (mask_first, mask_second):
            scores = dot_nt(query * mask, key) * (1.0 / 8.0)
            scores = jnp.where(valid, scores, -jnp.inf)
            grown = jnp.exp(scores - jnp.max(scores, axis=-1, keepdims=True))
            weights = grown / jnp.sum(grown, axis=-1, keepdims=True)
            halves.append(dot(weights.astype(BF16), value))
        parts.append(jnp.where(first, halves[0], halves[1]).astype(BF16))
    attended = jnp.concatenate(parts, axis=1)
    return x + dot(attended, w_out)


def kernel(
    tokens_hbm, gain_hbm, w_qkv_hbm, w_out_hbm, w_rec_hbm, solid_hbm,
    out_ref,
    tokens, gain, solid_ref, w_qkv, w_out, w_rec, send1, recv1, send2, near, far, row_halo,
    w_sel, main_w, side_w, edge_w, near_sel, far_sel, perm, edge_sel, row_sel,
    shifted, acc, edge_acc, ready,
    load_sem, send_sem, recv_sem, halo_send_sem, halo_recv_sem,
):
    i, k = lax.axis_index("row"), lax.axis_index("aisle")

    token_load = pltpu.make_async_copy(tokens_hbm, tokens, load_sem.at[6])
    token_load.start()
    loads = [
        pltpu.make_async_copy(gain_hbm, gain, load_sem.at[7]),
        pltpu.make_async_copy(w_qkv_hbm, w_qkv, load_sem.at[8]),
        pltpu.make_async_copy(w_out_hbm, w_out, load_sem.at[9]),
        pltpu.make_async_copy(solid_hbm, solid_ref, load_sem.at[10]),
    ]
    for load in loads:
        load.start()

    def rec_load(q):
        columns = pl.ds(pl.multiple_of(q * 1152, 1152), 1152)
        return pltpu.make_async_copy(w_rec_hbm.at[:, columns], w_rec.at[:, columns], load_sem.at[q])

    for q in range(6):
        rec_load(q).start()

    barrier = pltpu.get_barrier_semaphore()
    up, down = lax.rem(i + 1, N_ROW), lax.rem(i + N_ROW - 1, N_ROW)
    right, left = lax.rem(k + 1, N_AISLE), lax.rem(k + N_AISLE - 1, N_AISLE)
    has_up, has_down, has_right, has_left = i < N_ROW - 1, i > 0, k < N_AISLE - 1, k > 0
    gives_left, gives_right = (i < 2) & has_left, (i >= N_ROW - 2) & has_right

    @pl.loop(1, N_ROW)
    def _(step):
        pl.semaphore_signal(barrier, inc=1, device_id=(lax.rem(i + step, N_ROW), k), device_id_type=MESH)

    for present, column, first in ((has_left, left, N_ROW - 2), (has_right, right, 0)):
        @pl.when(present)
        def _():
            for j in (first, first + 1):
                pl.semaphore_signal(barrier, inc=1, device_id=(j, column), device_id_type=MESH)

    token_load.wait()
    mine = tokens[...].astype(F32).reshape(192, D).astype(BF16)
    send1[...] = dot(send_selector(), mine).reshape(32, 8, D).astype(BF16)
    recv1[i] = send1[i]
    pl.semaphore_wait(barrier, N_ROW - 1 + N_ROW * (gives_left.astype(I32) + gives_right.astype(I32)))

    def exchange(source, target, sem):
        @pl.loop(1, N_ROW)
        def _(step):
            j = lax.rem(i + step, N_ROW)
            pltpu.make_async_remote_copy(
                src_ref=source.at[j], dst_ref=target.at[i],
                send_sem=send_sem.at[sem], recv_sem=recv_sem.at[sem],
                device_id=(j, k), device_id_type=MESH,
            ).start()

    def drain(source, target, count, sem, start=0):
        return pltpu.make_async_remote_copy(
            src_ref=source.at[pl.ds(start, count)], dst_ref=target.at[pl.ds(start, count)],
            send_sem=send_sem.at[sem], recv_sem=recv_sem.at[sem],
            device_id=(lax.rem(i + 1, N_ROW), k), device_id_type=MESH,
        )

    exchange(send1, recv1, 0)

    @pl.loop(0, 8)
    def _(s):
        w_sel[s] = weight_selector(s)

    def prepare(q):
        rec_load(q).wait()
        for p in range(4):
            index = q * 4 + p
            c, pair = index // 6, index % 6
            found = []
            for s in (2 * p, 2 * p + 1):
                window = w_rec[:, pl.ds(pl.multiple_of(128 * (9 * q + s), 128), 256)]
                found.append(dot_nt(w_sel[s], window))
            main = [f[:64].reshape(8, 8, D) for f in found]
            main_w[c, :, pair] = jnp.concatenate(main, axis=1).astype(BF16)
            for side in range(2):
                at = 64 + 16 * side
                halves = [f[at : at + 16].reshape(2, 8, D) for f in found]
                side_w[side, c, :, pair] = jnp.concatenate(halves, axis=1).astype(BF16)
                for n in range(2):
                    for part in range(3):
                        at = 96 + 48 * side + 16 * part
                        edge_w[side, c, 2 * pair + n, :, part * D : (part + 1) * D] = found[n][at : at + 16].astype(BF16)

    @pl.loop(0, 3)
    def _(q):
        prepare(q)

    for load in loads:
        load.wait()
    drain(send1, recv1, N_ROW - 1, 0).wait_recv()

    x = recv1[...].astype(F32).reshape(256, D)
    block_out = attend_lines(x, gain[...], w_qkv[...], w_out[...])
    send2[...] = block_out.reshape(32, 8, D).astype(BF16)
    near[i] = send2[i]

    def give(present, column, group, sem):
        @pl.when(present)
        def _():
            @pl.loop(0, N_ROW)
            def _(step):
                j = lax.rem(i + step, N_ROW)
                pltpu.make_async_remote_copy(
                    src_ref=send2.at[j], dst_ref=near.at[group],
                    send_sem=halo_send_sem.at[sem], recv_sem=halo_recv_sem.at[sem],
                    device_id=(j, column), device_id_type=MESH,
                ).start()

    for row, group, given_to, column, sem in (
        (N_ROW - 2, 32, has_right, right, 0), (N_ROW - 1, 33, has_right, right, 0),
        (0, 34, has_left, left, 1), (1, 35, has_left, left, 1),
    ):
        give((i == row) & given_to, column, group, sem)
    exchange(send2, near, 1)

    row_sel[...] = row_halo_selector()
    perm[...] = lane_permutation()
    edge_sel[...] = edge_selector()
    for n, da in enumerate((0, -1, 1)):
        near_sel[n] = near_selector(da)
        far_sel[n] = far_selector(da)
    shifted[0] = jnp.zeros(shifted.shape[1:], BF16)
    shifted[5] = jnp.zeros(shifted.shape[1:], BF16)
    shifted[1:5, 4:6] = jnp.zeros((4, 2, 16, 3 * D), BF16)
    near[36:48] = jnp.zeros((12, 8, D), BF16)
    far[18:32] = jnp.zeros((14, 8, D), BF16)

    @pl.when(jnp.logical_not(has_left))
    def _():
        near[32:34] = jnp.zeros((2, 8, D), BF16)

    @pl.when(jnp.logical_not(has_right))
    def _():
        near[34:36] = jnp.zeros((2, 8, D), BF16)

    @pl.when(jnp.logical_not(has_down))
    def _():
        far[0:9] = jnp.zeros((9, 8, D), BF16)

    @pl.when(jnp.logical_not(has_up))
    def _():
        far[9:18] = jnp.zeros((9, 8, D), BF16)

    @pl.loop(3, 6)
    def _(q):
        prepare(q)

    drain(send1, recv1, N_ROW - 1, 0).wait_send()
    drain(send2, near, N_ROW - 1, 1).wait_recv()

    def given(count, group, sem):
        return pltpu.make_async_remote_copy(
            src_ref=send2.at[pl.ds(0, count)], dst_ref=near.at[pl.ds(group, count)],
            send_sem=halo_send_sem.at[sem], recv_sem=halo_recv_sem.at[sem],
            device_id=(lax.rem(i + 1, N_ROW), k), device_id_type=MESH,
        )

    @pl.when(has_left)
    def _():
        given(2, 32, 0).wait_recv()

    @pl.when(has_right)
    def _():
        given(2, 34, 1).wait_recv()

    gathered = near[...].astype(F32).reshape(384, D).astype(BF16)
    row_halo[...] = dot(row_sel[...], gathered).reshape(18, 8, D).astype(BF16)

    def row_copy(n):
        return pltpu.make_async_remote_copy(
            src_ref=row_halo.at[pl.ds(9 * n, 9)], dst_ref=far.at[pl.ds(9 - 9 * n, 9)],
            send_sem=halo_send_sem.at[2 + n], recv_sem=halo_recv_sem.at[2 + n],
            device_id=(up if n else down, k), device_id_type=MESH,
        )

    @pl.when(has_down)
    def _():
        row_copy(0).start()

    @pl.when(has_up)
    def _():
        row_copy(1).start()

    for n in range(3):
        picked = dot(near_sel[n], gathered).reshape(4, 3, 16, D).astype(BF16)
        shifted[1:5, 1:4, :, n * D : (n + 1) * D] = picked
    spans = ((0, 0, 8, 2), (-1, 0, 2, 10), (1, 6, 2, 0))
    for dz, z, n, kz in spans:
        here = pl.ds(1 + dz, 4)
        level = pl.ds(z, n)
        pairs = pl.ds(kz // 2, n // 2)
        token_part = shifted[here, 1:5, :, :D].reshape(256, D)
        found = dot_nt(main_w[:, :, pairs].reshape(-1, D), token_part).reshape(4, 8, n, 8, 256)
        if dz == 0:
            acc[...] = found
        else:
            acc[:, :, level] += found
        for side in range(2):
            token_part = shifted[here, 1:5, :, (side + 1) * D : (side + 2) * D].reshape(256, D)
            rows = side_w[side, :, :, pairs].reshape(-1, D)
            acc[:, pl.ds(6 * side, 2), level] += dot_nt(rows, token_part).reshape(4, 2, n, 8, 256)

    drain(send2, near, N_ROW - 1, 1).wait_send()
    for present, sem in ((gives_right, 0), (gives_left, 1)):
        @pl.when(present)
        def _():
            given(N_ROW, 0, sem).wait_send()

    for sends, comes, n in ((has_down, has_up, 0), (has_up, has_down, 1)):
        @pl.when(sends)
        def _():
            row_copy(n).wait_send()

        @pl.when(comes)
        def _():
            row_copy(n).wait_recv()

    gathered = far[...].astype(F32).reshape(256, D).astype(BF16)
    for n in range(3):
        picked = dot(far_sel[n], gathered).reshape(4, 2, 16, D).astype(BF16)
        shifted[1:5, 0, :, n * D : (n + 1) * D] = picked[:, 0]
        shifted[1:5, 4, :, n * D : (n + 1) * D] = picked[:, 1]

    for dz, z, n, kz in spans:
        for side in range(2):
            token_part = shifted[1 + dz : 5 + dz, 2 * side : 2 * side + 4].reshape(256, 3 * D)
            rows = edge_w[side, :, kz : kz + n].reshape(-1, 3 * D)
            found = dot_nt(rows, token_part).reshape(4, n, 16, 256)
            if dz == 0:
                edge_acc[:, :, side] = found
            else:
                edge_acc[:, z : z + n, side] += found
    for c in range(4):
        edges = edge_acc[c].reshape(256, 256).astype(BF16)
        total = acc[c].reshape(512, 256) + dot(edge_sel[...], edges)
        total = total.astype(BF16)
        for y in range(8):
            for b in range(2):
                ready[b, c, :, y * 128 : (y + 1) * 128] = total[y * 64 : (y + 1) * 64, b * 128 : (b + 1) * 128]
    solid = solid_ref[...]
    for low in range(2):
        cells = dot(ready[...].reshape(512, 1024), perm[:, low * 384 : (low + 1) * 384])
        for b in range(2):
            h = 2 * b + low
            part = cells[b * 256 : (b + 1) * 256]
            part = jnp.concatenate(
                [part[:, r * 128 : (r + 1) * 128].reshape(4, 8, 8, 128) for r in range(3)], axis=2
            )
            level = iota((4, 8, 24, 128), 1) + 8 * h
            out_ref[:, 8 * h : 8 * h + 8] = jnp.where(level < solid[None, None], 0.0, part).astype(BF16)


def body(tokens, ln_gain, w_qkv, w_out, w_rec, solid_top):
    vmem = pl.BlockSpec(memory_space=pltpu.VMEM)
    hbm = pl.BlockSpec(memory_space=pltpu.HBM)
    return pl.pallas_call(
        kernel,
        out_shape=jax.ShapeDtypeStruct((4, 32, 24, 128), BF16),
        in_specs=[hbm] * 6,
        out_specs=vmem,
        scratch_shapes=[
            pltpu.VMEM((3, 16, 4, D), BF16),
            pltpu.VMEM((1, D), F32),
            pltpu.VMEM((24, 128), I32),
            pltpu.VMEM((D, 3 * D), BF16),
            pltpu.VMEM((D, D), BF16),
            pltpu.VMEM((D, 6912), BF16),
            pltpu.VMEM((32, 8, D), BF16),
            pltpu.VMEM((32, 8, D), BF16),
            pltpu.VMEM((32, 8, D), BF16),
            pltpu.VMEM((48, 8, D), BF16),
            pltpu.VMEM((32, 8, D), BF16),
            pltpu.VMEM((18, 8, D), BF16),
            pltpu.VMEM((8, 192, 256), BF16),
            pltpu.VMEM((4, 8, 6, 16, D), BF16),
            pltpu.VMEM((2, 4, 2, 6, 16, D), BF16),
            pltpu.VMEM((2, 4, 12, 16, 3 * D), BF16),
            pltpu.VMEM((3, 192, 384), BF16),
            pltpu.VMEM((3, 128, 256), BF16),
            pltpu.VMEM((1024, 768), BF16),
            pltpu.VMEM((512, 256), BF16),
            pltpu.VMEM((144, 384), BF16),
            pltpu.VMEM((6, 6, 16, 3 * D), BF16),
            pltpu.VMEM((4, 8, 8, 8, 256), F32),
            pltpu.VMEM((4, 8, 2, 16, 256), F32),
            pltpu.VMEM((2, 4, 64, 1024), BF16),
            pltpu.SemaphoreType.DMA((11,)),
            pltpu.SemaphoreType.DMA((2,)),
            pltpu.SemaphoreType.DMA((2,)),
            pltpu.SemaphoreType.DMA((4,)),
            pltpu.SemaphoreType.DMA((4,)),
        ],
        compiler_params=pltpu.CompilerParams(
            collective_id=0, has_side_effects=True, vmem_limit_bytes=60 * 1024 * 1024
        ),
        cost_estimate=pl.CostEstimate(flops=6 * 10**9, bytes_accessed=11 * 10**6, transcendentals=2**19),
        name="airflow_block",
    )(tokens, ln_gain.reshape(1, D), w_qkv, w_out, w_rec, solid_top)


def solution(mesh):
    in_specs = (P("row", "aisle", None, None), P(), P(), P(), P(), P("row", "aisle"))
    out_specs = P(None, None, "row", "aisle")
    return jax.shard_map(body, mesh=mesh, in_specs=in_specs, out_specs=out_specs, check_vma=False)
```

```python
import jax
import jax.numpy as jnp
from jax import lax
from jax.experimental import pallas as pl
from jax.experimental.pallas import tpu as pltpu
from jax.sharding import PartitionSpec as P

EPSILON = 1e-05
N_ROW, N_AISLE = 32, 8
D, HEADS, DH = 512, 8, 64
MESH = pl.DeviceIdType.MESH
F32, BF16, I32 = jnp.float32, jnp.bfloat16, jnp.int32


def iota(shape, dim):
    return lax.broadcasted_iota(I32, shape, dim)


def one_hot(hit):
    return jnp.where(hit, 1.0, 0.0).astype(BF16)


def dot(a, b):
    return lax.dot_general(a, b, (((1,), (0,)), ((), ())), preferred_element_type=F32)


def dot_nt(a, b):
    return lax.dot_general(a, b, (((1,), (1,)), ((), ())), preferred_element_type=F32)


def send_selector():
    row = iota((256, 1), 0)
    pair = ((row >> 3) & 15) * 2 + (row >> 7)
    source = (row & 3) * 64 + pair * 2 + ((row >> 2) & 1)
    source = jnp.where((row & 3) < 3, source, -1)
    return one_hot(iota((256, 192), 1) == source)


def weight_selector(step):
    row = iota((192, 1), 0)
    main = ((row & 7) + 2) * 12 + (row >> 3) + 2
    below = ((row & 7) + 2) * 12 + ((row >> 3) & 1) + 10
    above = ((row & 7) + 2) * 12 + ((row >> 3) & 1)
    edge = row - 96
    side = jnp.where(edge >= 48, 1, 0)
    edge = edge - 48 * side
    part = edge >> 4
    y = (edge >> 1) & 7
    x = edge & 1
    kx = jnp.where(side == 0, x + 10, x)
    ky = jnp.where(
        part == 0,
        y + 2,
        jnp.where(
            part == 1, jnp.where(y < 2, y + 10, -999), jnp.where(y >= 6, y - 6, -999)
        ),
    )
    edged = kx * 12 + ky
    column = jnp.where(row < 64, main, jnp.where(row < 80, below, jnp.where(row < 96, above, edged)))
    return one_hot(iota((192, 256), 1) - 16 * step == column)


def near_selector(da):
    q = iota((192, 1), 0)
    h = jnp.where(q >= 144, 3, jnp.where(q >= 96, 2, jnp.where(q >= 48, 1, 0)))
    rest = q - 48 * h
    r, a = rest >> 4, (rest & 15) + da
    block = jnp.where(a < 0, 16, jnp.where(a > 15, 17, a))
    return one_hot(iota((192, 384), 1) == block * 16 + h * 4 + r)


def far_selector(da):
    q = iota((128, 1), 0)
    h, side, a = q >> 5, (q >> 4) & 1, (q & 15) + da
    block = jnp.where(a < 0, 16, jnp.where(a > 15, 17, a))
    return one_hot(iota((128, 256), 1) == side * 72 + block * 4 + h)


def lane_permutation():
    row = iota((1024, 1), 0)
    r = (row >> 4) & 3
    target = ((row >> 6) & 1) * 384 + r * 128 + (row & 15) * 8 + (row >> 7)
    target = jnp.where(r < 3, target, -1)
    return one_hot(iota((1024, 768), 1) == target)


def edge_selector():
    column = iota((1, 256), 1)
    target = (
        ((column >> 1) & 7) * 64 + (column >> 5) * 8 + ((column >> 4) & 1) * 6 + (column & 1)
    )
    return one_hot(iota((512, 256), 0) == target)


def row_halo_selector():
    row = iota((144, 1), 0)
    source = jnp.where(row >= 72, (row - 72) * 4 + 2, row * 4)
    return one_hot(iota((144, 384), 1) == source)


def attend_lines(x, gain, w_qkv, w_out):
    center = x - jnp.mean(x, axis=-1, keepdims=True)
    spread = jnp.mean(center * center, axis=-1, keepdims=True)
    normed = (center * lax.rsqrt(spread + EPSILON) * gain).astype(BF16)
    qkv = dot(normed, w_qkv).astype(BF16)
    rows, cols = iota((256, 256), 0), iota((256, 256), 1)
    valid = (((rows ^ cols) & 4) == 0) & ((cols & 3) < 3)
    first = iota((256, 128), 1) < DH
    mask_first = one_hot(first)
    mask_second = 1 - mask_first
    parts = []
    for pair in range(HEADS // 2):
        at = pair * 2 * DH
        query = qkv[:, at : at + 2 * DH]
        key = qkv[:, D + at : D + at + 2 * DH]
        value = qkv[:, 2 * D + at : 2 * D + at + 2 * DH]
        halves = []
        for mask in (mask_first, mask_second):
            scores = dot_nt(query * mask, key) * (1.0 / 8.0)
            scores = jnp.where(valid, scores, -jnp.inf)
            grown = jnp.exp(scores - jnp.max(scores, axis=-1, keepdims=True))
            weights = grown / jnp.sum(grown, axis=-1, keepdims=True)
            halves.append(dot(weights.astype(BF16), value))
        parts.append(jnp.where(first, halves[0], halves[1]).astype(BF16))
    attended = jnp.concatenate(parts, axis=1)
    return x + dot(attended, w_out)


def kernel(
    tokens_hbm, gain_hbm, w_qkv_hbm, w_out_hbm, w_rec_hbm, solid_hbm,
    out_ref,
    tokens, gain, solid_ref, w_qkv, w_out, w_rec, send1, recv1, send2, near, far, row_halo,
    w_sel, main_w, side_w, edge_w, near_sel, far_sel, perm, edge_sel, row_sel,
    shifted, acc, edge_acc, ready,
    load_sem, send_sem, recv_sem, halo_send_sem, halo_recv_sem,
):
    i, k = lax.axis_index("row"), lax.axis_index("aisle")

    token_load = pltpu.make_async_copy(tokens_hbm, tokens, load_sem.at[6])
    token_load.start()
    loads = [
        pltpu.make_async_copy(gain_hbm, gain, load_sem.at[7]),
        pltpu.make_async_copy(w_qkv_hbm, w_qkv, load_sem.at[8]),
        pltpu.make_async_copy(w_out_hbm, w_out, load_sem.at[9]),
        pltpu.make_async_copy(solid_hbm, solid_ref, load_sem.at[10]),
    ]
    for load in loads:
        load.start()

    def rec_load(q):
        columns = pl.ds(pl.multiple_of(q * 1152, 1152), 1152)
        return pltpu.make_async_copy(w_rec_hbm.at[:, columns], w_rec.at[:, columns], load_sem.at[q])

    for q in range(6):
        rec_load(q).start()

    barrier = pltpu.get_barrier_semaphore()
    up, down = lax.rem(i + 1, N_ROW), lax.rem(i + N_ROW - 1, N_ROW)
    right, left = lax.rem(k + 1, N_AISLE), lax.rem(k + N_AISLE - 1, N_AISLE)
    has_up, has_down, has_right, has_left = i < N_ROW - 1, i > 0, k < N_AISLE - 1, k > 0
    pair = lax.rem(i, 16) * 2 + lax.div(i, 16)
    gives_left, gives_right = (lax.rem(i, 16) == 0) & has_left, (lax.rem(i, 16) == 15) & has_right

    @pl.loop(1, N_ROW)
    def _(step):
        pl.semaphore_signal(barrier, inc=1, device_id=(lax.rem(i + step, N_ROW), k), device_id_type=MESH)

    for present, column, first in ((has_left, left, 15), (has_right, right, 0)):
        @pl.when(present)
        def _():
            for j in (first, first + 16):
                pl.semaphore_signal(barrier, inc=1, device_id=(j, column), device_id_type=MESH)

    token_load.wait()
    mine = tokens[...].astype(F32).reshape(192, D).astype(BF16)
    send1[...] = dot(send_selector(), mine).reshape(32, 8, D).astype(BF16)
    recv1[i] = send1[i]
    pl.semaphore_wait(barrier, N_ROW - 1 + N_ROW * (gives_left.astype(I32) + gives_right.astype(I32)))

    def exchange(source, target, place, sem):
        @pl.loop(1, N_ROW)
        def _(step):
            j = lax.rem(i + step, N_ROW)
            pltpu.make_async_remote_copy(
                src_ref=source.at[j], dst_ref=target.at[place],
                send_sem=send_sem.at[sem], recv_sem=recv_sem.at[sem],
                device_id=(j, k), device_id_type=MESH,
            ).start()

    def drain(source, target, count, sem, start=0):
        return pltpu.make_async_remote_copy(
            src_ref=source.at[pl.ds(start, count)], dst_ref=target.at[pl.ds(start, count)],
            send_sem=send_sem.at[sem], recv_sem=recv_sem.at[sem],
            device_id=(lax.rem(i + 1, N_ROW), k), device_id_type=MESH,
        )

    exchange(send1, recv1, i, 0)

    @pl.loop(0, 8)
    def _(s):
        w_sel[s] = weight_selector(s)

    def prepare(q):
        rec_load(q).wait()
        for p in range(4):
            index = q * 4 + p
            c, pair = index // 6, index % 6
            found = []
            for s in (2 * p, 2 * p + 1):
                window = w_rec[:, pl.ds(pl.multiple_of(128 * (9 * q + s), 128), 256)]
                found.append(dot_nt(w_sel[s], window))
            main = [f[:64].reshape(8, 8, D) for f in found]
            main_w[c, :, pair] = jnp.concatenate(main, axis=1).astype(BF16)
            for side in range(2):
                at = 64 + 16 * side
                halves = [f[at : at + 16].reshape(2, 8, D) for f in found]
                side_w[side, c, :, pair] = jnp.concatenate(halves, axis=1).astype(BF16)
                for n in range(2):
                    for part in range(3):
                        at = 96 + 48 * side + 16 * part
                        edge_w[side, c, 2 * pair + n, :, part * D : (part + 1) * D] = found[n][at : at + 16].astype(BF16)

    @pl.loop(0, 3)
    def _(q):
        prepare(q)

    for load in loads:
        load.wait()
    drain(send1, recv1, N_ROW - 1, 0).wait_recv()

    x = recv1[...].astype(F32).reshape(256, D)
    block_out = attend_lines(x, gain[...], w_qkv[...], w_out[...])
    send2[...] = block_out.reshape(32, 8, D).astype(BF16)
    near[pair] = send2[i]

    def give(present, column, group, sem):
        @pl.when(present)
        def _():
            @pl.loop(0, N_ROW)
            def _(step):
                j = lax.rem(i + step, N_ROW)
                pltpu.make_async_remote_copy(
                    src_ref=send2.at[j], dst_ref=near.at[group],
                    send_sem=halo_send_sem.at[sem], recv_sem=halo_recv_sem.at[sem],
                    device_id=(j, column), device_id_type=MESH,
                ).start()

    for row, group, given_to, column, sem in (
        (15, 32, has_right, right, 0), (31, 33, has_right, right, 0),
        (0, 34, has_left, left, 1), (16, 35, has_left, left, 1),
    ):
        give((i == row) & given_to, column, group, sem)
    exchange(send2, near, pair, 1)

    row_sel[...] = row_halo_selector()
    perm[...] = lane_permutation()
    edge_sel[...] = edge_selector()
    for n, da in enumerate((0, -1, 1)):
        near_sel[n] = near_selector(da)
        far_sel[n] = far_selector(da)
    shifted[0] = jnp.zeros(shifted.shape[1:], BF16)
    shifted[5] = jnp.zeros(shifted.shape[1:], BF16)
    shifted[1:5, 4:6] = jnp.zeros((4, 2, 16, 3 * D), BF16)
    near[36:48] = jnp.zeros((12, 8, D), BF16)
    far[18:32] = jnp.zeros((14, 8, D), BF16)

    @pl.when(jnp.logical_not(has_left))
    def _():
        near[32:34] = jnp.zeros((2, 8, D), BF16)

    @pl.when(jnp.logical_not(has_right))
    def _():
        near[34:36] = jnp.zeros((2, 8, D), BF16)

    @pl.when(jnp.logical_not(has_down))
    def _():
        far[0:9] = jnp.zeros((9, 8, D), BF16)

    @pl.when(jnp.logical_not(has_up))
    def _():
        far[9:18] = jnp.zeros((9, 8, D), BF16)

    @pl.loop(3, 6)
    def _(q):
        prepare(q)

    drain(send1, recv1, N_ROW - 1, 0).wait_send()
    drain(send2, near, N_ROW - 1, 1).wait_recv()

    def given(count, group, sem):
        return pltpu.make_async_remote_copy(
            src_ref=send2.at[pl.ds(0, count)], dst_ref=near.at[pl.ds(group, count)],
            send_sem=halo_send_sem.at[sem], recv_sem=halo_recv_sem.at[sem],
            device_id=(lax.rem(i + 1, N_ROW), k), device_id_type=MESH,
        )

    @pl.when(has_left)
    def _():
        given(2, 32, 0).wait_recv()

    @pl.when(has_right)
    def _():
        given(2, 34, 1).wait_recv()

    gathered = near[...].astype(F32).reshape(384, D).astype(BF16)
    row_halo[...] = dot(row_sel[...], gathered).reshape(18, 8, D).astype(BF16)

    def row_copy(n):
        return pltpu.make_async_remote_copy(
            src_ref=row_halo.at[pl.ds(9 * n, 9)], dst_ref=far.at[pl.ds(9 - 9 * n, 9)],
            send_sem=halo_send_sem.at[2 + n], recv_sem=halo_recv_sem.at[2 + n],
            device_id=(up if n else down, k), device_id_type=MESH,
        )

    @pl.when(has_down)
    def _():
        row_copy(0).start()

    @pl.when(has_up)
    def _():
        row_copy(1).start()

    for n in range(3):
        picked = dot(near_sel[n], gathered).reshape(4, 3, 16, D).astype(BF16)
        shifted[1:5, 1:4, :, n * D : (n + 1) * D] = picked
    spans = ((0, 0, 8, 2), (-1, 0, 2, 10), (1, 6, 2, 0))
    for dz, z, n, kz in spans:
        here = pl.ds(1 + dz, 4)
        level = pl.ds(z, n)
        pairs = pl.ds(kz // 2, n // 2)
        token_part = shifted[here, 1:5, :, :D].reshape(256, D)
        found = dot_nt(main_w[:, :, pairs].reshape(-1, D), token_part).reshape(4, 8, n, 8, 256)
        if dz == 0:
            acc[...] = found
        else:
            acc[:, :, level] += found
        for side in range(2):
            token_part = shifted[here, 1:5, :, (side + 1) * D : (side + 2) * D].reshape(256, D)
            rows = side_w[side, :, :, pairs].reshape(-1, D)
            acc[:, pl.ds(6 * side, 2), level] += dot_nt(rows, token_part).reshape(4, 2, n, 8, 256)

    drain(send2, near, N_ROW - 1, 1).wait_send()
    for present, sem in ((gives_right, 0), (gives_left, 1)):
        @pl.when(present)
        def _():
            given(N_ROW, 0, sem).wait_send()

    for sends, comes, n in ((has_down, has_up, 0), (has_up, has_down, 1)):
        @pl.when(sends)
        def _():
            row_copy(n).wait_send()

        @pl.when(comes)
        def _():
            row_copy(n).wait_recv()

    gathered = far[...].astype(F32).reshape(256, D).astype(BF16)
    for n in range(3):
        picked = dot(far_sel[n], gathered).reshape(4, 2, 16, D).astype(BF16)
        shifted[1:5, 0, :, n * D : (n + 1) * D] = picked[:, 0]
        shifted[1:5, 4, :, n * D : (n + 1) * D] = picked[:, 1]

    for dz, z, n, kz in spans:
        for side in range(2):
            token_part = shifted[1 + dz : 5 + dz, 2 * side : 2 * side + 4].reshape(256, 3 * D)
            rows = edge_w[side, :, kz : kz + n].reshape(-1, 3 * D)
            found = dot_nt(rows, token_part).reshape(4, n, 16, 256)
            if dz == 0:
                edge_acc[:, :, side] = found
            else:
                edge_acc[:, z : z + n, side] += found
    for c in range(4):
        edges = edge_acc[c].reshape(256, 256).astype(BF16)
        total = acc[c].reshape(512, 256) + dot(edge_sel[...], edges)
        total = total.astype(BF16)
        for y in range(8):
            for b in range(2):
                ready[b, c, :, y * 128 : (y + 1) * 128] = total[y * 64 : (y + 1) * 64, b * 128 : (b + 1) * 128]
    solid = solid_ref[...]
    for low in range(2):
        cells = dot(ready[...].reshape(512, 1024), perm[:, low * 384 : (low + 1) * 384])
        for b in range(2):
            h = 2 * b + low
            part = cells[b * 256 : (b + 1) * 256]
            part = jnp.concatenate(
                [part[:, r * 128 : (r + 1) * 128].reshape(4, 8, 8, 128) for r in range(3)], axis=2
            )
            level = iota((4, 8, 24, 128), 1) + 8 * h
            out_ref[:, 8 * h : 8 * h + 8] = jnp.where(level < solid[None, None], 0.0, part).astype(BF16)


def body(tokens, ln_gain, w_qkv, w_out, w_rec, solid_top):
    vmem = pl.BlockSpec(memory_space=pltpu.VMEM)
    hbm = pl.BlockSpec(memory_space=pltpu.HBM)
    return pl.pallas_call(
        kernel,
        out_shape=jax.ShapeDtypeStruct((4, 32, 24, 128), BF16),
        in_specs=[hbm] * 6,
        out_specs=vmem,
        scratch_shapes=[
            pltpu.VMEM((3, 16, 4, D), BF16),
            pltpu.VMEM((1, D), F32),
            pltpu.VMEM((24, 128), I32),
            pltpu.VMEM((D, 3 * D), BF16),
            pltpu.VMEM((D, D), BF16),
            pltpu.VMEM((D, 6912), BF16),
            pltpu.VMEM((32, 8, D), BF16),
            pltpu.VMEM((32, 8, D), BF16),
            pltpu.VMEM((32, 8, D), BF16),
            pltpu.VMEM((48, 8, D), BF16),
            pltpu.VMEM((32, 8, D), BF16),
            pltpu.VMEM((18, 8, D), BF16),
            pltpu.VMEM((8, 192, 256), BF16),
            pltpu.VMEM((4, 8, 6, 16, D), BF16),
            pltpu.VMEM((2, 4, 2, 6, 16, D), BF16),
            pltpu.VMEM((2, 4, 12, 16, 3 * D), BF16),
            pltpu.VMEM((3, 192, 384), BF16),
            pltpu.VMEM((3, 128, 256), BF16),
            pltpu.VMEM((1024, 768), BF16),
            pltpu.VMEM((512, 256), BF16),
            pltpu.VMEM((144, 384), BF16),
            pltpu.VMEM((6, 6, 16, 3 * D), BF16),
            pltpu.VMEM((4, 8, 8, 8, 256), F32),
            pltpu.VMEM((4, 8, 2, 16, 256), F32),
            pltpu.VMEM((2, 4, 64, 1024), BF16),
            pltpu.SemaphoreType.DMA((11,)),
            pltpu.SemaphoreType.DMA((2,)),
            pltpu.SemaphoreType.DMA((2,)),
            pltpu.SemaphoreType.DMA((4,)),
            pltpu.SemaphoreType.DMA((4,)),
        ],
        compiler_params=pltpu.CompilerParams(
            collective_id=0, has_side_effects=True, vmem_limit_bytes=60 * 1024 * 1024
        ),
        cost_estimate=pl.CostEstimate(flops=6 * 10**9, bytes_accessed=11 * 10**6, transcendentals=2**19),
        name="airflow_block",
    )(tokens, ln_gain.reshape(1, D), w_qkv, w_out, w_rec, solid_top)


def solution(mesh):
    in_specs = (P("row", "aisle", None, None), P(), P(), P(), P(), P("row", "aisle"))
    out_specs = P(None, None, "row", "aisle")
    return jax.shard_map(body, mesh=mesh, in_specs=in_specs, out_specs=out_specs, check_vma=False)
```

```python
import jax
import jax.numpy as jnp
from jax import lax
from jax.experimental import pallas as pl
from jax.experimental.pallas import tpu as pltpu
from jax.sharding import PartitionSpec as P

EPSILON = 1e-05
N_ROW, N_AISLE = 32, 8
D, HEADS, DH = 512, 8, 64
MESH = pl.DeviceIdType.MESH
F32, BF16, I32 = jnp.float32, jnp.bfloat16, jnp.int32


def iota(shape, dim):
    return lax.broadcasted_iota(I32, shape, dim)


def one_hot(hit):
    return jnp.where(hit, 1.0, 0.0).astype(BF16)


def dot(a, b):
    return lax.dot_general(a, b, (((1,), (0,)), ((), ())), preferred_element_type=F32)


def dot_nt(a, b):
    return lax.dot_general(a, b, (((1,), (1,)), ((), ())), preferred_element_type=F32)


def send_selector():
    row = iota((256, 1), 0)
    pair = ((row >> 3) & 15) * 2 + (row >> 7)
    source = (row & 3) * 64 + pair * 2 + ((row >> 2) & 1)
    source = jnp.where((row & 3) < 3, source, -1)
    return one_hot(iota((256, 192), 1) == source)


def weight_selector(step):
    row = iota((192, 1), 0)
    main = ((row & 7) + 2) * 12 + (row >> 3) + 2
    below = ((row & 7) + 2) * 12 + ((row >> 3) & 1) + 10
    above = ((row & 7) + 2) * 12 + ((row >> 3) & 1)
    edge = row - 96
    side = jnp.where(edge >= 48, 1, 0)
    edge = edge - 48 * side
    part = edge >> 4
    y = (edge >> 1) & 7
    x = edge & 1
    kx = jnp.where(side == 0, x + 10, x)
    ky = jnp.where(
        part == 0,
        y + 2,
        jnp.where(
            part == 1, jnp.where(y < 2, y + 10, -999), jnp.where(y >= 6, y - 6, -999)
        ),
    )
    edged = kx * 12 + ky
    column = jnp.where(row < 64, main, jnp.where(row < 80, below, jnp.where(row < 96, above, edged)))
    return one_hot(iota((192, 256), 1) - 16 * step == column)


def near_selector(da):
    q = iota((192, 1), 0)
    h = jnp.where(q >= 144, 3, jnp.where(q >= 96, 2, jnp.where(q >= 48, 1, 0)))
    rest = q - 48 * h
    r, a = rest >> 4, (rest & 15) + da
    block = jnp.where(a < 0, 16, jnp.where(a > 15, 17, a))
    return one_hot(iota((192, 384), 1) == block * 16 + h * 4 + r)


def far_selector(da):
    q = iota((128, 1), 0)
    h, side, a = q >> 5, (q >> 4) & 1, (q & 15) + da
    block = jnp.where(a < 0, 16, jnp.where(a > 15, 17, a))
    return one_hot(iota((128, 256), 1) == side * 72 + block * 4 + h)


def lane_permutation():
    row = iota((1024, 1), 0)
    r = (row >> 4) & 3
    target = ((row >> 6) & 1) * 384 + r * 128 + (row & 15) * 8 + (row >> 7)
    target = jnp.where(r < 3, target, -1)
    return one_hot(iota((1024, 768), 1) == target)


def edge_selector():
    column = iota((1, 256), 1)
    target = (
        ((column >> 1) & 7) * 64 + (column >> 5) * 8 + ((column >> 4) & 1) * 6 + (column & 1)
    )
    return one_hot(iota((512, 256), 0) == target)


def row_halo_selector():
    row = iota((144, 1), 0)
    source = jnp.where(row >= 72, (row - 72) * 4 + 2, row * 4)
    return one_hot(iota((144, 384), 1) == source)


def attend_lines(x, gain, w_qkv, w_out):
    center = x - jnp.mean(x, axis=-1, keepdims=True)
    spread = jnp.mean(center * center, axis=-1, keepdims=True)
    normed = (center * lax.rsqrt(spread + EPSILON) * gain).astype(BF16)
    qkv = dot(normed, w_qkv).astype(BF16)
    rows, cols = iota((256, 256), 0), iota((256, 256), 1)
    valid = (((rows ^ cols) & 4) == 0) & ((cols & 3) < 3)
    first = iota((256, 128), 1) < DH
    mask_first = one_hot(first)
    mask_second = 1 - mask_first
    parts = []
    for pair in range(HEADS // 2):
        at = pair * 2 * DH
        query = qkv[:, at : at + 2 * DH]
        key = qkv[:, D + at : D + at + 2 * DH]
        value = qkv[:, 2 * D + at : 2 * D + at + 2 * DH]
        halves = []
        for mask in (mask_first, mask_second):
            scores = dot_nt(query * mask, key) * (1.0 / 8.0)
            scores = jnp.where(valid, scores, -jnp.inf)
            grown = jnp.exp(scores - jnp.max(scores, axis=-1, keepdims=True))
            total = jnp.sum(grown, axis=-1, keepdims=True)
            halves.append(dot(grown.astype(BF16), value) / total)
        parts.append(jnp.where(first, halves[0], halves[1]).astype(BF16))
    attended = jnp.concatenate(parts, axis=1)
    return x + dot(attended, w_out)


def kernel(
    tokens_hbm, gain_hbm, w_qkv_hbm, w_out_hbm, w_rec_hbm, solid_hbm,
    out_ref,
    tokens, gain, solid_ref, w_qkv, w_out, w_rec, send1, recv1, send2, near, far, row_halo,
    w_sel, main_w, side_w, edge_w, near_sel, far_sel, perm, edge_sel, row_sel,
    shifted, acc, edge_acc, ready,
    load_sem, send_sem, recv_sem, halo_send_sem, halo_recv_sem,
):
    i, k = lax.axis_index("row"), lax.axis_index("aisle")

    token_load = pltpu.make_async_copy(tokens_hbm, tokens, load_sem.at[6])
    token_load.start()
    loads = [
        pltpu.make_async_copy(gain_hbm, gain, load_sem.at[7]),
        pltpu.make_async_copy(w_qkv_hbm, w_qkv, load_sem.at[8]),
        pltpu.make_async_copy(w_out_hbm, w_out, load_sem.at[9]),
        pltpu.make_async_copy(solid_hbm, solid_ref, load_sem.at[10]),
    ]
    for load in loads:
        load.start()

    def rec_load(q):
        columns = pl.ds(pl.multiple_of(q * 1152, 1152), 1152)
        return pltpu.make_async_copy(w_rec_hbm.at[:, columns], w_rec.at[:, columns], load_sem.at[q])

    for q in range(6):
        rec_load(q).start()

    barrier = pltpu.get_barrier_semaphore()
    up, down = lax.rem(i + 1, N_ROW), lax.rem(i + N_ROW - 1, N_ROW)
    right, left = lax.rem(k + 1, N_AISLE), lax.rem(k + N_AISLE - 1, N_AISLE)
    has_up, has_down, has_right, has_left = i < N_ROW - 1, i > 0, k < N_AISLE - 1, k > 0
    pair = lax.rem(i, 16) * 2 + lax.div(i, 16)
    gives_left, gives_right = (lax.rem(i, 16) == 0) & has_left, (lax.rem(i, 16) == 15) & has_right

    @pl.loop(1, N_ROW)
    def _(step):
        pl.semaphore_signal(barrier, inc=1, device_id=(lax.rem(i + step, N_ROW), k), device_id_type=MESH)

    for present, column, first in ((has_left, left, 15), (has_right, right, 0)):
        @pl.when(present)
        def _():
            for j in (first, first + 16):
                pl.semaphore_signal(barrier, inc=1, device_id=(j, column), device_id_type=MESH)

    token_load.wait()
    mine = tokens[...].astype(F32).reshape(192, D).astype(BF16)
    send1[...] = dot(send_selector(), mine).reshape(32, 8, D).astype(BF16)
    recv1[i] = send1[i]
    pl.semaphore_wait(barrier, N_ROW - 1 + N_ROW * (gives_left.astype(I32) + gives_right.astype(I32)))

    def exchange(source, target, place, sem):
        @pl.loop(1, N_ROW)
        def _(step):
            j = lax.rem(i + step, N_ROW)
            pltpu.make_async_remote_copy(
                src_ref=source.at[j], dst_ref=target.at[place],
                send_sem=send_sem.at[sem], recv_sem=recv_sem.at[sem],
                device_id=(j, k), device_id_type=MESH,
            ).start()

    def drain(source, target, count, sem, start=0):
        return pltpu.make_async_remote_copy(
            src_ref=source.at[pl.ds(start, count)], dst_ref=target.at[pl.ds(start, count)],
            send_sem=send_sem.at[sem], recv_sem=recv_sem.at[sem],
            device_id=(lax.rem(i + 1, N_ROW), k), device_id_type=MESH,
        )

    exchange(send1, recv1, i, 0)

    @pl.loop(0, 8)
    def _(s):
        w_sel[s] = weight_selector(s)

    def prepare(q):
        rec_load(q).wait()
        for p in range(4):
            index = q * 4 + p
            c, pair = index // 6, index % 6
            found = []
            for s in (2 * p, 2 * p + 1):
                window = w_rec[:, pl.ds(pl.multiple_of(128 * (9 * q + s), 128), 256)]
                found.append(dot_nt(w_sel[s], window))
            main = [f[:64].reshape(8, 8, D) for f in found]
            main_w[c, :, pair] = jnp.concatenate(main, axis=1).astype(BF16)
            for side in range(2):
                at = 64 + 16 * side
                halves = [f[at : at + 16].reshape(2, 8, D) for f in found]
                side_w[side, c, :, pair] = jnp.concatenate(halves, axis=1).astype(BF16)
                for n in range(2):
                    for part in range(3):
                        at = 96 + 48 * side + 16 * part
                        edge_w[side, c, 2 * pair + n, :, part * D : (part + 1) * D] = found[n][at : at + 16].astype(BF16)

    @pl.loop(0, 3)
    def _(q):
        prepare(q)

    for load in loads:
        load.wait()
    drain(send1, recv1, N_ROW - 1, 0).wait_recv()

    x = recv1[...].astype(F32).reshape(256, D)
    block_out = attend_lines(x, gain[...], w_qkv[...], w_out[...])
    send2[...] = block_out.reshape(32, 8, D).astype(BF16)
    near[pair] = send2[i]

    def give(present, column, group, sem):
        @pl.when(present)
        def _():
            @pl.loop(0, N_ROW)
            def _(step):
                j = lax.rem(i + step, N_ROW)
                pltpu.make_async_remote_copy(
                    src_ref=send2.at[j], dst_ref=near.at[group],
                    send_sem=halo_send_sem.at[sem], recv_sem=halo_recv_sem.at[sem],
                    device_id=(j, column), device_id_type=MESH,
                ).start()

    for row, group, given_to, column, sem in (
        (15, 32, has_right, right, 0), (31, 33, has_right, right, 0),
        (0, 34, has_left, left, 1), (16, 35, has_left, left, 1),
    ):
        give((i == row) & given_to, column, group, sem)
    exchange(send2, near, pair, 1)

    row_sel[...] = row_halo_selector()
    perm[...] = lane_permutation()
    edge_sel[...] = edge_selector()
    for n, da in enumerate((0, -1, 1)):
        near_sel[n] = near_selector(da)
        far_sel[n] = far_selector(da)
    shifted[:, 4:6] = jnp.zeros((4, 2, 16, 3 * D), BF16)
    near[36:48] = jnp.zeros((12, 8, D), BF16)
    far[18:32] = jnp.zeros((14, 8, D), BF16)

    @pl.when(jnp.logical_not(has_left))
    def _():
        near[32:34] = jnp.zeros((2, 8, D), BF16)

    @pl.when(jnp.logical_not(has_right))
    def _():
        near[34:36] = jnp.zeros((2, 8, D), BF16)

    @pl.when(jnp.logical_not(has_down))
    def _():
        far[0:9] = jnp.zeros((9, 8, D), BF16)

    @pl.when(jnp.logical_not(has_up))
    def _():
        far[9:18] = jnp.zeros((9, 8, D), BF16)

    @pl.loop(3, 6)
    def _(q):
        prepare(q)

    drain(send1, recv1, N_ROW - 1, 0).wait_send()
    drain(send2, near, N_ROW - 1, 1).wait_recv()

    def given(count, group, sem):
        return pltpu.make_async_remote_copy(
            src_ref=send2.at[pl.ds(0, count)], dst_ref=near.at[pl.ds(group, count)],
            send_sem=halo_send_sem.at[sem], recv_sem=halo_recv_sem.at[sem],
            device_id=(lax.rem(i + 1, N_ROW), k), device_id_type=MESH,
        )

    @pl.when(has_left)
    def _():
        given(2, 32, 0).wait_recv()

    @pl.when(has_right)
    def _():
        given(2, 34, 1).wait_recv()

    gathered = near[...].astype(F32).reshape(384, D).astype(BF16)
    row_halo[...] = dot(row_sel[...], gathered).reshape(18, 8, D).astype(BF16)

    def row_copy(n):
        return pltpu.make_async_remote_copy(
            src_ref=row_halo.at[pl.ds(9 * n, 9)], dst_ref=far.at[pl.ds(9 - 9 * n, 9)],
            send_sem=halo_send_sem.at[2 + n], recv_sem=halo_recv_sem.at[2 + n],
            device_id=(up if n else down, k), device_id_type=MESH,
        )

    @pl.when(has_down)
    def _():
        row_copy(0).start()

    @pl.when(has_up)
    def _():
        row_copy(1).start()

    for n in range(3):
        picked = dot(near_sel[n], gathered).reshape(4, 3, 16, D).astype(BF16)
        shifted[:, 1:4, :, n * D : (n + 1) * D] = picked
    lane = iota((1, 256), 1)

    def from_below(values):
        return jnp.where(lane >= 64, pltpu.roll(values.reshape(-1, 256), 64, 1), 0.0).reshape(values.shape)

    def from_above(values):
        return jnp.where(lane < 192, pltpu.roll(values.reshape(-1, 256), 192, 1), 0.0).reshape(values.shape)

    found = dot_nt(main_w[...].reshape(-1, D), shifted[:, 1:5, :, :D].reshape(256, D)).reshape(4, 8, 12, 8, 256)
    acc[...] = found[:, :, 2:10]
    acc[:, :, 0:2] += from_below(found[:, :, 10:12])
    acc[:, :, 6:8] += from_above(found[:, :, 0:2])
    for side in range(2):
        token_part = shifted[:, 1:5, :, (side + 1) * D : (side + 2) * D].reshape(256, D)
        found = dot_nt(side_w[side].reshape(-1, D), token_part).reshape(4, 2, 12, 8, 256)
        rows = pl.ds(6 * side, 2)
        acc[:, rows] += found[:, :, 2:10]
        acc[:, rows, 0:2] += from_below(found[:, :, 10:12])
        acc[:, rows, 6:8] += from_above(found[:, :, 0:2])

    drain(send2, near, N_ROW - 1, 1).wait_send()
    for present, sem in ((gives_right, 0), (gives_left, 1)):
        @pl.when(present)
        def _():
            given(N_ROW, 0, sem).wait_send()

    for sends, comes, n in ((has_down, has_up, 0), (has_up, has_down, 1)):
        @pl.when(sends)
        def _():
            row_copy(n).wait_send()

        @pl.when(comes)
        def _():
            row_copy(n).wait_recv()

    gathered = far[...].astype(F32).reshape(256, D).astype(BF16)
    for n in range(3):
        picked = dot(far_sel[n], gathered).reshape(4, 2, 16, D).astype(BF16)
        shifted[:, 0, :, n * D : (n + 1) * D] = picked[:, 0]
        shifted[:, 4, :, n * D : (n + 1) * D] = picked[:, 1]

    for side in range(2):
        token_part = shifted[:, 2 * side : 2 * side + 4].reshape(256, 3 * D)
        found = dot_nt(edge_w[side].reshape(-1, 3 * D), token_part).reshape(4, 12, 16, 256)
        edge_acc[:, :, side] = found[:, 2:10]
        edge_acc[:, 0:2, side] += from_below(found[:, 10:12])
        edge_acc[:, 6:8, side] += from_above(found[:, 0:2])

    solid = solid_ref[...]
    insides = [iota((8, 24, 128), 0) + 8 * h < solid[None] for h in range(4)]
    for first_c in range(0, 4, 2):
        lines = []
        for c in range(first_c, first_c + 2):
            edges = edge_acc[c].reshape(256, 256).astype(BF16)
            total = acc[c].reshape(512, 256) + dot(edge_sel[...], edges)
            for b in range(2):
                lines.append(jnp.concatenate(
                    [total[y * 64 : (y + 1) * 64, b * 128 : (b + 1) * 128] for y in range(8)], axis=1
                ))
        cells = dot(jnp.concatenate(lines, axis=0).astype(BF16), perm[...])
        for n in range(2):
            for h in range(4):
                b, low = h // 2, h % 2
                part = cells[128 * n + b * 64 : 128 * n + (b + 1) * 64]
                part = jnp.concatenate(
                    [part[:, low * 384 + r * 128 : low * 384 + (r + 1) * 128].reshape(8, 8, 128) for r in range(3)], axis=1
                )
                out_ref[first_c + n, 8 * h : 8 * h + 8] = jnp.where(insides[h], 0.0, part).astype(BF16)


def body(tokens, ln_gain, w_qkv, w_out, w_rec, solid_top):
    vmem = pl.BlockSpec(memory_space=pltpu.VMEM)
    hbm = pl.BlockSpec(memory_space=pltpu.HBM)
    return pl.pallas_call(
        kernel,
        out_shape=jax.ShapeDtypeStruct((4, 32, 24, 128), BF16),
        in_specs=[hbm] * 6,
        out_specs=vmem,
        scratch_shapes=[
            pltpu.VMEM((3, 16, 4, D), BF16),
            pltpu.VMEM((1, D), F32),
            pltpu.VMEM((24, 128), I32),
            pltpu.VMEM((D, 3 * D), BF16),
            pltpu.VMEM((D, D), BF16),
            pltpu.VMEM((D, 6912), BF16),
            pltpu.VMEM((32, 8, D), BF16),
            pltpu.VMEM((32, 8, D), BF16),
            pltpu.VMEM((32, 8, D), BF16),
            pltpu.VMEM((48, 8, D), BF16),
            pltpu.VMEM((32, 8, D), BF16),
            pltpu.VMEM((18, 8, D), BF16),
            pltpu.VMEM((8, 192, 256), BF16),
            pltpu.VMEM((4, 8, 6, 16, D), BF16),
            pltpu.VMEM((2, 4, 2, 6, 16, D), BF16),
            pltpu.VMEM((2, 4, 12, 16, 3 * D), BF16),
            pltpu.VMEM((3, 192, 384), BF16),
            pltpu.VMEM((3, 128, 256), BF16),
            pltpu.VMEM((1024, 768), BF16),
            pltpu.VMEM((512, 256), BF16),
            pltpu.VMEM((144, 384), BF16),
            pltpu.VMEM((4, 6, 16, 3 * D), BF16),
            pltpu.VMEM((4, 8, 8, 8, 256), F32),
            pltpu.VMEM((4, 8, 2, 16, 256), F32),
            pltpu.VMEM((2, 4, 64, 1024), BF16),
            pltpu.SemaphoreType.DMA((11,)),
            pltpu.SemaphoreType.DMA((2,)),
            pltpu.SemaphoreType.DMA((2,)),
            pltpu.SemaphoreType.DMA((4,)),
            pltpu.SemaphoreType.DMA((4,)),
        ],
        compiler_params=pltpu.CompilerParams(
            collective_id=0, has_side_effects=True, vmem_limit_bytes=60 * 1024 * 1024
        ),
        cost_estimate=pl.CostEstimate(flops=6 * 10**9, bytes_accessed=11 * 10**6, transcendentals=2**19),
        name="airflow_block",
    )(tokens, ln_gain.reshape(1, D), w_qkv, w_out, w_rec, solid_top)


def solution(mesh):
    in_specs = (P("row", "aisle", None, None), P(), P(), P(), P(), P("row", "aisle"))
    out_specs = P(None, None, "row", "aisle")
    return jax.shard_map(body, mesh=mesh, in_specs=in_specs, out_specs=out_specs, check_vma=False)
```

```python
import jax
import jax.numpy as jnp
from jax import lax
from jax.experimental import pallas as pl
from jax.experimental.pallas import tpu as pltpu
from jax.sharding import PartitionSpec as P

EPSILON = 1e-05
N_ROW, N_AISLE = 32, 8
D, HEADS, DH = 512, 8, 64
MESH = pl.DeviceIdType.MESH
F32, BF16, I32 = jnp.float32, jnp.bfloat16, jnp.int32


def iota(shape, dim):
    return lax.broadcasted_iota(I32, shape, dim)


def one_hot(hit):
    return jnp.where(hit, 1.0, 0.0).astype(BF16)


def dot(a, b):
    return lax.dot_general(a, b, (((1,), (0,)), ((), ())), preferred_element_type=F32)


def dot_nt(a, b):
    return lax.dot_general(a, b, (((1,), (1,)), ((), ())), preferred_element_type=F32)


def send_selector():
    row = iota((256, 1), 0)
    pair = ((row >> 3) & 15) * 2 + (row >> 7)
    source = (row & 3) * 64 + pair * 2 + ((row >> 2) & 1)
    source = jnp.where((row & 3) < 3, source, -1)
    return one_hot(iota((256, 192), 1) == source)


def weight_selector(step):
    row = iota((192, 1), 0)
    main = ((row & 7) + 2) * 12 + (row >> 3) + 2
    below = ((row & 7) + 2) * 12 + ((row >> 3) & 1) + 10
    above = ((row & 7) + 2) * 12 + ((row >> 3) & 1)
    edge = row - 96
    side = jnp.where(edge >= 48, 1, 0)
    edge = edge - 48 * side
    part = edge >> 4
    y = (edge >> 1) & 7
    x = edge & 1
    kx = jnp.where(side == 0, x + 10, x)
    ky = jnp.where(
        part == 0,
        y + 2,
        jnp.where(
            part == 1, jnp.where(y < 2, y + 10, -999), jnp.where(y >= 6, y - 6, -999)
        ),
    )
    edged = kx * 12 + ky
    column = jnp.where(row < 64, main, jnp.where(row < 80, below, jnp.where(row < 96, above, edged)))
    return one_hot(iota((192, 256), 1) - 16 * step == column)


def near_selector(da):
    q = iota((256, 1), 0)
    h, r, a = q >> 6, (q >> 4) & 3, (q & 15) + da
    block = jnp.where(a < 0, 16, jnp.where(a > 15, 17, a))
    return one_hot(iota((256, 384), 1) == block * 16 + h * 4 + r)


def far_selector(da):
    q = iota((64, 1), 0)
    h, a = q >> 4, (q & 15) + da
    block = jnp.where(a < 0, 16, jnp.where(a > 15, 17, a))
    return one_hot(iota((64, 128), 1) == block * 4 + h)


def slot_selector():
    row = iota((256, 1), 0)
    i, slot = row >> 3, row & 3
    beside = jnp.where((i & 1) == 0, row - 9, row + 5)
    beside = jnp.where((i == 0) | (i == N_ROW - 1), -1, beside)
    return one_hot(iota((256, 256), 1) == jnp.where(slot < 3, row, beside))


def lane_permutation():
    row = iota((1024, 1), 0)
    r = (row >> 4) & 3
    target = ((row >> 6) & 1) * 384 + r * 128 + (row & 15) * 8 + (row >> 7)
    target = jnp.where(r < 3, target, -1)
    return one_hot(iota((1024, 768), 1) == target)


def edge_selector():
    column = iota((1, 256), 1)
    target = (
        ((column >> 1) & 7) * 64 + (column >> 5) * 8 + ((column >> 4) & 1) * 6 + (column & 1)
    )
    return one_hot(iota((512, 256), 0) == target)


def row_halo_selector(core):
    row = iota((80, 1), 0)
    source = jnp.where(row < 72, row * 4 + 2 - 2 * core, -1)
    return one_hot(iota((80, 384), 1) == source)


def attend_lines(x, gain, w_qkv, w_out):
    center = x - jnp.mean(x, axis=-1, keepdims=True)
    spread = jnp.mean(center * center, axis=-1, keepdims=True)
    normed = (center * lax.rsqrt(spread + EPSILON) * gain).astype(BF16)
    qkv = dot(normed, w_qkv).astype(BF16)
    rows, cols = iota((256, 256), 0), iota((256, 256), 1)
    valid = (((rows ^ cols) & 4) == 0) & ((cols & 3) < 3)
    first = iota((256, 128), 1) < DH
    mask_first = one_hot(first)
    mask_second = 1 - mask_first
    parts = []
    for pair in range(HEADS // 2):
        at = pair * 2 * DH
        query = qkv[:, at : at + 2 * DH]
        key = qkv[:, D + at : D + at + 2 * DH]
        value = qkv[:, 2 * D + at : 2 * D + at + 2 * DH]
        halves = []
        for mask in (mask_first, mask_second):
            scores = dot_nt(query * mask, key) * (1.0 / 8.0)
            scores = jnp.where(valid, scores, -jnp.inf)
            grown = jnp.exp(scores - jnp.max(scores, axis=-1, keepdims=True))
            total = jnp.sum(grown, axis=-1, keepdims=True)
            halves.append(dot(grown.astype(BF16), value) / total)
        parts.append(jnp.where(first, halves[0], halves[1]).astype(BF16))
    attended = jnp.concatenate(parts, axis=1)
    return x + dot(attended, w_out)


def kernel(
    tokens_hbm, gain_hbm, w_qkv_hbm, w_out_hbm, w_rec_hbm, solid_hbm,
    out_ref,
    tokens, gain, solid_ref, w_qkv, w_out, w_rec, send1, recv1, send2, near, far, row_halo,
    w_sel, main_w, side_w, edge_w, near_sel, far_sel, perm, edge_sel, row_sel, slot_sel,
    shifted, acc, edge_acc, ready,
    load_sem, send_sem, recv_sem, halo_send_sem, halo_recv_sem,
):
    i, k = lax.axis_index("row"), lax.axis_index("aisle")

    token_load = pltpu.make_async_copy(tokens_hbm, tokens, load_sem.at[6])
    token_load.start()
    loads = [
        pltpu.make_async_copy(gain_hbm, gain, load_sem.at[7]),
        pltpu.make_async_copy(w_qkv_hbm, w_qkv, load_sem.at[8]),
        pltpu.make_async_copy(w_out_hbm, w_out, load_sem.at[9]),
        pltpu.make_async_copy(solid_hbm, solid_ref, load_sem.at[10]),
    ]
    for load in loads:
        load.start()

    def rec_load(q):
        columns = pl.ds(pl.multiple_of(q * 1152, 1152), 1152)
        return pltpu.make_async_copy(w_rec_hbm.at[:, columns], w_rec.at[:, columns], load_sem.at[q])

    for q in range(6):
        rec_load(q).start()

    barrier = pltpu.get_barrier_semaphore()
    core = lax.rem(i, 2)
    partner = i + 1 - 2 * core
    right, left = lax.rem(k + 1, N_AISLE), lax.rem(k + N_AISLE - 1, N_AISLE)
    has_right, has_left = k < N_AISLE - 1, k > 0
    pair = lax.rem(i, 16) * 2 + lax.div(i, 16)
    gives_left, gives_right = (lax.rem(i, 16) == 0) & has_left, (lax.rem(i, 16) == 15) & has_right

    @pl.loop(1, N_ROW)
    def _(step):
        pl.semaphore_signal(barrier, inc=1, device_id=(lax.rem(i + step, N_ROW), k), device_id_type=MESH)

    for present, column, first in ((has_left, left, 15), (has_right, right, 0)):
        @pl.when(present)
        def _():
            for j in (first, first + 16):
                pl.semaphore_signal(barrier, inc=1, device_id=(j, column), device_id_type=MESH)

    token_load.wait()
    mine = tokens[...].astype(F32).reshape(192, D).astype(BF16)
    send1[...] = dot(send_selector(), mine).reshape(32, 8, D).astype(BF16)
    recv1[i] = send1[i]
    pl.semaphore_wait(barrier, N_ROW - 1 + N_ROW * (gives_left.astype(I32) + gives_right.astype(I32)))

    def exchange(source, target, place, sem):
        @pl.loop(1, N_ROW)
        def _(step):
            j = lax.rem(i + step, N_ROW)
            pltpu.make_async_remote_copy(
                src_ref=source.at[j], dst_ref=target.at[place],
                send_sem=send_sem.at[sem], recv_sem=recv_sem.at[sem],
                device_id=(j, k), device_id_type=MESH,
            ).start()

    def drain(source, target, count, sem, start=0):
        return pltpu.make_async_remote_copy(
            src_ref=source.at[pl.ds(start, count)], dst_ref=target.at[pl.ds(start, count)],
            send_sem=send_sem.at[sem], recv_sem=recv_sem.at[sem],
            device_id=(lax.rem(i + 1, N_ROW), k), device_id_type=MESH,
        )

    exchange(send1, recv1, i, 0)

    @pl.loop(0, 8)
    def _(s):
        w_sel[s] = weight_selector(s)

    def prepare(q):
        rec_load(q).wait()
        for p in range(4):
            index = q * 4 + p
            c, pair = index // 6, index % 6
            found = []
            for s in (2 * p, 2 * p + 1):
                window = w_rec[:, pl.ds(pl.multiple_of(128 * (9 * q + s), 128), 256)]
                found.append(dot_nt(w_sel[s], window))
            main = [f[:64].reshape(8, 8, D) for f in found]
            main_w[c, :, pair] = jnp.concatenate(main, axis=1).astype(BF16)
            for side in range(2):
                at = 64 + 16 * side
                halves = [f[at : at + 16].reshape(2, 8, D) for f in found]
                side_w[side, c, :, pair] = jnp.concatenate(halves, axis=1).astype(BF16)
                for n in range(2):
                    for part in range(3):
                        at = 96 + 48 * side + 16 * part
                        edge_w[side, c, 2 * pair + n, :, part * D : (part + 1) * D] = found[n][at : at + 16].astype(BF16)

    slot_sel[...] = slot_selector()

    @pl.loop(0, 3)
    def _(q):
        prepare(q)

    for load in loads:
        load.wait()
    drain(send1, recv1, N_ROW - 1, 0).wait_recv()

    x = recv1[...].astype(F32).reshape(256, D)
    block_out = attend_lines(x, gain[...], w_qkv[...], w_out[...])
    send2[...] = dot(slot_sel[...], block_out.astype(BF16)).reshape(32, 8, D).astype(BF16)
    near[pair] = send2[i]

    def give(present, column, group, sem):
        @pl.when(present)
        def _():
            @pl.loop(0, N_ROW)
            def _(step):
                j = lax.rem(i + step, N_ROW)
                pltpu.make_async_remote_copy(
                    src_ref=send2.at[j], dst_ref=near.at[group],
                    send_sem=halo_send_sem.at[sem], recv_sem=halo_recv_sem.at[sem],
                    device_id=(j, column), device_id_type=MESH,
                ).start()

    for row, group, given_to, column, sem in (
        (15, 32, has_right, right, 0), (31, 33, has_right, right, 0),
        (0, 34, has_left, left, 1), (16, 35, has_left, left, 1),
    ):
        give((i == row) & given_to, column, group, sem)
    exchange(send2, near, pair, 1)

    row_sel[...] = row_halo_selector(core)
    perm[...] = lane_permutation()
    edge_sel[...] = edge_selector()
    for n, da in enumerate((0, -1, 1)):
        near_sel[n] = near_selector(da)
        far_sel[n] = far_selector(da)
    shifted[:, 4:6] = jnp.zeros((4, 2, 16, 3 * D), BF16)
    near[36:48] = jnp.zeros((12, 8, D), BF16)
    far[9:16] = jnp.zeros((7, 8, D), BF16)

    @pl.when(jnp.logical_not(has_left))
    def _():
        near[32:34] = jnp.zeros((2, 8, D), BF16)

    @pl.when(jnp.logical_not(has_right))
    def _():
        near[34:36] = jnp.zeros((2, 8, D), BF16)

    @pl.loop(3, 6)
    def _(q):
        prepare(q)

    drain(send1, recv1, N_ROW - 1, 0).wait_send()
    drain(send2, near, N_ROW - 1, 1).wait_recv()

    def given(count, group, sem):
        return pltpu.make_async_remote_copy(
            src_ref=send2.at[pl.ds(0, count)], dst_ref=near.at[pl.ds(group, count)],
            send_sem=halo_send_sem.at[sem], recv_sem=halo_recv_sem.at[sem],
            device_id=(lax.rem(i + 1, N_ROW), k), device_id_type=MESH,
        )

    @pl.when(has_left)
    def _():
        given(2, 32, 0).wait_recv()

    @pl.when(has_right)
    def _():
        given(2, 34, 1).wait_recv()

    gathered = near[...].astype(F32).reshape(384, D).astype(BF16)
    row_halo[...] = dot(row_sel[...], gathered).reshape(10, 8, D).astype(BF16)
    row_copy = pltpu.make_async_remote_copy(
        src_ref=row_halo.at[pl.ds(0, 9)], dst_ref=far.at[pl.ds(0, 9)],
        send_sem=halo_send_sem.at[2], recv_sem=halo_recv_sem.at[2],
        device_id=(partner, k), device_id_type=MESH,
    )
    row_copy.start()

    for n in range(3):
        picked = dot(near_sel[n], gathered).reshape(4, 4, 16, D).astype(BF16)
        shifted[:, 1:4, :, n * D : (n + 1) * D] = picked[:, 0:3]
        shifted[:, pl.ds(4 * core, 1), :, n * D : (n + 1) * D] = picked[:, 3:4]
    lane = iota((1, 256), 1)

    def from_below(values):
        return jnp.where(lane >= 64, pltpu.roll(values.reshape(-1, 256), 64, 1), 0.0).reshape(values.shape)

    def from_above(values):
        return jnp.where(lane < 192, pltpu.roll(values.reshape(-1, 256), 192, 1), 0.0).reshape(values.shape)

    found = dot_nt(main_w[...].reshape(-1, D), shifted[:, 1:5, :, :D].reshape(256, D)).reshape(4, 8, 12, 8, 256)
    acc[...] = found[:, :, 2:10]
    acc[:, :, 0:2] += from_below(found[:, :, 10:12])
    acc[:, :, 6:8] += from_above(found[:, :, 0:2])
    for side in range(2):
        token_part = shifted[:, 1:5, :, (side + 1) * D : (side + 2) * D].reshape(256, D)
        found = dot_nt(side_w[side].reshape(-1, D), token_part).reshape(4, 2, 12, 8, 256)
        rows = pl.ds(6 * side, 2)
        acc[:, rows] += found[:, :, 2:10]
        acc[:, rows, 0:2] += from_below(found[:, :, 10:12])
        acc[:, rows, 6:8] += from_above(found[:, :, 0:2])

    drain(send2, near, N_ROW - 1, 1).wait_send()
    for present, sem in ((gives_right, 0), (gives_left, 1)):
        @pl.when(present)
        def _():
            given(N_ROW, 0, sem).wait_send()

    row_copy.wait()

    gathered = far[...].astype(F32).reshape(128, D).astype(BF16)
    for n in range(3):
        picked = dot(far_sel[n], gathered).reshape(4, 1, 16, D).astype(BF16)
        shifted[:, pl.ds(4 - 4 * core, 1), :, n * D : (n + 1) * D] = picked

    for side in range(2):
        token_part = shifted[:, 2 * side : 2 * side + 4].reshape(256, 3 * D)
        found = dot_nt(edge_w[side].reshape(-1, 3 * D), token_part).reshape(4, 12, 16, 256)
        edge_acc[:, :, side] = found[:, 2:10]
        edge_acc[:, 0:2, side] += from_below(found[:, 10:12])
        edge_acc[:, 6:8, side] += from_above(found[:, 0:2])

    solid = solid_ref[...]
    insides = [iota((8, 24, 128), 0) + 8 * h < solid[None] for h in range(4)]
    for first_c in range(0, 4, 2):
        lines = []
        for c in range(first_c, first_c + 2):
            edges = edge_acc[c].reshape(256, 256).astype(BF16)
            total = acc[c].reshape(512, 256) + dot(edge_sel[...], edges)
            for b in range(2):
                lines.append(jnp.concatenate(
                    [total[y * 64 : (y + 1) * 64, b * 128 : (b + 1) * 128] for y in range(8)], axis=1
                ))
        cells = dot(jnp.concatenate(lines, axis=0).astype(BF16), perm[...])
        for n in range(2):
            for h in range(4):
                b, low = h // 2, h % 2
                part = cells[128 * n + b * 64 : 128 * n + (b + 1) * 64]
                part = jnp.concatenate(
                    [part[:, low * 384 + r * 128 : low * 384 + (r + 1) * 128].reshape(8, 8, 128) for r in range(3)], axis=1
                )
                out_ref[first_c + n, 8 * h : 8 * h + 8] = jnp.where(insides[h], 0.0, part).astype(BF16)


def body(tokens, ln_gain, w_qkv, w_out, w_rec, solid_top):
    vmem = pl.BlockSpec(memory_space=pltpu.VMEM)
    hbm = pl.BlockSpec(memory_space=pltpu.HBM)
    return pl.pallas_call(
        kernel,
        out_shape=jax.ShapeDtypeStruct((4, 32, 24, 128), BF16),
        in_specs=[hbm] * 6,
        out_specs=vmem,
        scratch_shapes=[
            pltpu.VMEM((3, 16, 4, D), BF16),
            pltpu.VMEM((1, D), F32),
            pltpu.VMEM((24, 128), I32),
            pltpu.VMEM((D, 3 * D), BF16),
            pltpu.VMEM((D, D), BF16),
            pltpu.VMEM((D, 6912), BF16),
            pltpu.VMEM((32, 8, D), BF16),
            pltpu.VMEM((32, 8, D), BF16),
            pltpu.VMEM((32, 8, D), BF16),
            pltpu.VMEM((48, 8, D), BF16),
            pltpu.VMEM((16, 8, D), BF16),
            pltpu.VMEM((10, 8, D), BF16),
            pltpu.VMEM((8, 192, 256), BF16),
            pltpu.VMEM((4, 8, 6, 16, D), BF16),
            pltpu.VMEM((2, 4, 2, 6, 16, D), BF16),
            pltpu.VMEM((2, 4, 12, 16, 3 * D), BF16),
            pltpu.VMEM((3, 256, 384), BF16),
            pltpu.VMEM((3, 64, 128), BF16),
            pltpu.VMEM((1024, 768), BF16),
            pltpu.VMEM((512, 256), BF16),
            pltpu.VMEM((80, 384), BF16),
            pltpu.VMEM((256, 256), BF16),
            pltpu.VMEM((4, 6, 16, 3 * D), BF16),
            pltpu.VMEM((4, 8, 8, 8, 256), F32),
            pltpu.VMEM((4, 8, 2, 16, 256), F32),
            pltpu.VMEM((2, 4, 64, 1024), BF16),
            pltpu.SemaphoreType.DMA((11,)),
            pltpu.SemaphoreType.DMA((2,)),
            pltpu.SemaphoreType.DMA((2,)),
            pltpu.SemaphoreType.DMA((4,)),
            pltpu.SemaphoreType.DMA((4,)),
        ],
        compiler_params=pltpu.CompilerParams(
            collective_id=0, has_side_effects=True, vmem_limit_bytes=60 * 1024 * 1024
        ),
        cost_estimate=pl.CostEstimate(flops=6 * 10**9, bytes_accessed=11 * 10**6, transcendentals=2**19),
        name="airflow_block",
    )(tokens, ln_gain.reshape(1, D), w_qkv, w_out, w_rec, solid_top)


def solution(mesh):
    in_specs = (P("row", "aisle", None, None), P(), P(), P(), P(), P("row", "aisle"))
    out_specs = P(None, None, "row", "aisle")
    return jax.shard_map(body, mesh=mesh, in_specs=in_specs, out_specs=out_specs, check_vma=False)
```

```python
import jax
import jax.numpy as jnp
from jax import lax
from jax.experimental import pallas as pl
from jax.experimental.pallas import tpu as pltpu
from jax.sharding import PartitionSpec as P

EPSILON = 1e-05
N_ROW, N_AISLE = 32, 8
D, HEADS, DH = 512, 8, 64
MESH = pl.DeviceIdType.MESH
F32, BF16, I32 = jnp.float32, jnp.bfloat16, jnp.int32


def iota(shape, dim):
    return lax.broadcasted_iota(I32, shape, dim)


def one_hot(hit):
    return jnp.where(hit, 1.0, 0.0).astype(BF16)


def dot(a, b):
    return lax.dot_general(a, b, (((1,), (0,)), ((), ())), preferred_element_type=F32)


def dot_nt(a, b):
    return lax.dot_general(a, b, (((1,), (1,)), ((), ())), preferred_element_type=F32)


def send_selector():
    row = iota((256, 1), 0)
    pair = ((row >> 3) & 15) * 2 + (row >> 7)
    source = (row & 3) * 64 + pair * 2 + ((row >> 2) & 1)
    source = jnp.where((row & 3) < 3, source, -1)
    return one_hot(iota((256, 192), 1) == source)


def weight_selector(step):
    row = iota((192, 1), 0)
    main = ((row & 7) + 2) * 12 + (row >> 3) + 2
    below = ((row & 7) + 2) * 12 + ((row >> 3) & 1) + 10
    above = ((row & 7) + 2) * 12 + ((row >> 3) & 1)
    edge = row - 96
    side = jnp.where(edge >= 48, 1, 0)
    edge = edge - 48 * side
    part = edge >> 4
    y = (edge >> 1) & 7
    x = edge & 1
    kx = jnp.where(side == 0, x + 10, x)
    ky = jnp.where(
        part == 0,
        y + 2,
        jnp.where(
            part == 1, jnp.where(y < 2, y + 10, -999), jnp.where(y >= 6, y - 6, -999)
        ),
    )
    edged = kx * 12 + ky
    column = jnp.where(row < 64, main, jnp.where(row < 80, below, jnp.where(row < 96, above, edged)))
    return one_hot(iota((192, 256), 1) - 16 * step == column)


def near_selector(da):
    q = iota((256, 1), 0)
    h, r, a = q >> 6, (q >> 4) & 3, (q & 15) + da
    block = jnp.where(a < 0, 16, jnp.where(a > 15, 17, a))
    return one_hot(iota((256, 384), 1) == block * 16 + h * 4 + r)


def far_selector(da):
    q = iota((64, 1), 0)
    h, a = q >> 4, (q & 15) + da
    block = jnp.where(a < 0, 16, jnp.where(a > 15, 17, a))
    return one_hot(iota((64, 128), 1) == block * 4 + h)


def slot_selector():
    row = iota((256, 1), 0)
    i, slot = row >> 3, row & 3
    beside = jnp.where((i & 1) == 0, row - 9, row + 5)
    beside = jnp.where((i == 0) | (i == N_ROW - 1), -1, beside)
    return one_hot(iota((256, 256), 1) == jnp.where(slot < 3, row, beside))


def lane_permutation():
    row = iota((1024, 1), 0)
    r = (row >> 4) & 3
    target = ((row >> 6) & 1) * 384 + r * 128 + (row & 15) * 8 + (row >> 7)
    target = jnp.where(r < 3, target, -1)
    return one_hot(iota((1024, 768), 1) == target)


def edge_selector():
    column = iota((1, 256), 1)
    target = (
        ((column >> 1) & 7) * 64 + (column >> 5) * 8 + ((column >> 4) & 1) * 6 + (column & 1)
    )
    return one_hot(iota((512, 256), 0) == target)


def row_halo_selector(core):
    row = iota((80, 1), 0)
    source = jnp.where(row < 72, row * 4 + 2 - 2 * core, -1)
    return one_hot(iota((80, 384), 1) == source)


def attend_lines(x, gain, w_qkv, w_out):
    center = x - jnp.mean(x, axis=-1, keepdims=True)
    spread = jnp.mean(center * center, axis=-1, keepdims=True)
    normed = (center * lax.rsqrt(spread + EPSILON) * gain).astype(BF16)
    qkv = dot(normed, w_qkv).astype(BF16)
    rows, cols = iota((256, 256), 0), iota((256, 256), 1)
    valid = (((rows ^ cols) & 4) == 0) & ((cols & 3) < 3)
    first = iota((256, 128), 1) < DH
    mask_first = one_hot(first)
    mask_second = 1 - mask_first
    parts = []
    for pair in range(HEADS // 2):
        at = pair * 2 * DH
        query = qkv[:, at : at + 2 * DH]
        key = qkv[:, D + at : D + at + 2 * DH]
        value = qkv[:, 2 * D + at : 2 * D + at + 2 * DH]
        halves = []
        for mask in (mask_first, mask_second):
            scores = dot_nt(query * mask, key) * (1.0 / 8.0)
            scores = jnp.where(valid, scores, -jnp.inf)
            grown = jnp.exp(scores - jnp.max(scores, axis=-1, keepdims=True))
            total = jnp.sum(grown, axis=-1, keepdims=True)
            halves.append(dot(grown.astype(BF16), value) / total)
        parts.append(jnp.where(first, halves[0], halves[1]).astype(BF16))
    attended = jnp.concatenate(parts, axis=1)
    return x + dot(attended, w_out)


def kernel(
    tokens_hbm, gain_hbm, w_qkv_hbm, w_out_hbm, w_rec_hbm, solid_hbm,
    out_ref,
    tokens, gain, solid_ref, w_qkv, w_out, w_rec, send1, recv1, send2, near, far, row_halo,
    w_sel, main_w, side_w, edge_w, near_sel, far_sel, perm, edge_sel, row_sel, slot_sel,
    shifted, acc, edge_acc, ready,
    load_sem, send_sem, recv_sem, halo_send_sem, halo_recv_sem,
):
    i, k = lax.axis_index("row"), lax.axis_index("aisle")

    token_load = pltpu.make_async_copy(tokens_hbm, tokens, load_sem.at[6])
    token_load.start()
    loads = [
        pltpu.make_async_copy(gain_hbm, gain, load_sem.at[7]),
        pltpu.make_async_copy(w_qkv_hbm, w_qkv, load_sem.at[8]),
        pltpu.make_async_copy(w_out_hbm, w_out, load_sem.at[9]),
        pltpu.make_async_copy(solid_hbm, solid_ref, load_sem.at[10]),
    ]
    for load in loads:
        load.start()

    def rec_load(q):
        columns = pl.ds(pl.multiple_of(q * 1152, 1152), 1152)
        return pltpu.make_async_copy(w_rec_hbm.at[:, columns], w_rec.at[:, columns], load_sem.at[q])

    for q in range(6):
        rec_load(q).start()

    barrier = pltpu.get_barrier_semaphore()
    core = lax.rem(i, 2)
    partner = i + 1 - 2 * core
    right, left = lax.rem(k + 1, N_AISLE), lax.rem(k + N_AISLE - 1, N_AISLE)
    has_right, has_left = k < N_AISLE - 1, k > 0
    pair = lax.rem(i, 16) * 2 + lax.div(i, 16)
    gives_left, gives_right = (lax.rem(i, 16) == 0) & has_left, (lax.rem(i, 16) == 15) & has_right

    @pl.loop(1, N_ROW)
    def _(step):
        pl.semaphore_signal(barrier, inc=1, device_id=(lax.rem(i + step, N_ROW), k), device_id_type=MESH)

    for present, column, first in ((has_left, left, 15), (has_right, right, 0)):
        @pl.when(present)
        def _():
            for j in (first, first + 16):
                pl.semaphore_signal(barrier, inc=1, device_id=(j, column), device_id_type=MESH)

    token_load.wait()
    mine = tokens[...].astype(F32).reshape(192, D).astype(BF16)
    send1[...] = dot(send_selector(), mine).reshape(32, 8, D).astype(BF16)
    recv1[i] = send1[i]
    pl.semaphore_wait(barrier, N_ROW - 1 + N_ROW * (gives_left.astype(I32) + gives_right.astype(I32)))

    def exchange(source, target, place, sem):
        @pl.loop(1, N_ROW)
        def _(step):
            j = lax.rem(i + step, N_ROW)
            pltpu.make_async_remote_copy(
                src_ref=source.at[j], dst_ref=target.at[place],
                send_sem=send_sem.at[sem], recv_sem=recv_sem.at[sem],
                device_id=(j, k), device_id_type=MESH,
            ).start()

    def drain(source, target, count, sem, start=0):
        return pltpu.make_async_remote_copy(
            src_ref=source.at[pl.ds(start, count)], dst_ref=target.at[pl.ds(start, count)],
            send_sem=send_sem.at[sem], recv_sem=recv_sem.at[sem],
            device_id=(lax.rem(i + 1, N_ROW), k), device_id_type=MESH,
        )

    exchange(send1, recv1, i, 0)

    @pl.loop(0, 8)
    def _(s):
        w_sel[s] = weight_selector(s)

    def prepare(q):
        rec_load(q).wait()
        for p in range(4):
            index = q * 4 + p
            c, pair = index // 6, index % 6
            found = []
            for s in (2 * p, 2 * p + 1):
                window = w_rec[:, pl.ds(pl.multiple_of(128 * (9 * q + s), 128), 256)]
                found.append(dot_nt(w_sel[s], window))
            main = [f[:64].reshape(8, 8, D) for f in found]
            main_w[c, :, pair] = jnp.concatenate(main, axis=1).astype(BF16)
            for side in range(2):
                at = 64 + 16 * side
                halves = [f[at : at + 16].reshape(2, 8, D) for f in found]
                side_w[side, c, :, pair] = jnp.concatenate(halves, axis=1).astype(BF16)
                for n in range(2):
                    for part in range(3):
                        at = 96 + 48 * side + 16 * part
                        edge_w[side, c, 2 * pair + n, :, part * D : (part + 1) * D] = found[n][at : at + 16].astype(BF16)

    slot_sel[...] = slot_selector()

    @pl.loop(0, 3)
    def _(q):
        prepare(q)

    for load in loads:
        load.wait()
    drain(send1, recv1, N_ROW - 1, 0).wait_recv()

    x = recv1[...].astype(F32).reshape(256, D)
    block_out = attend_lines(x, gain[...], w_qkv[...], w_out[...])
    send2[...] = dot(slot_sel[...], block_out.astype(BF16)).reshape(32, 8, D).astype(BF16)
    near[pair] = send2[i]

    def give(present, column, group, sem):
        @pl.when(present)
        def _():
            @pl.loop(0, N_ROW)
            def _(step):
                j = lax.rem(i + step, N_ROW)
                pltpu.make_async_remote_copy(
                    src_ref=send2.at[j], dst_ref=near.at[group],
                    send_sem=halo_send_sem.at[sem], recv_sem=halo_recv_sem.at[sem],
                    device_id=(j, column), device_id_type=MESH,
                ).start()

    exchange(send2, near, pair, 1)
    for row, group, given_to, column, sem in (
        (15, 32, has_right, right, 0), (31, 33, has_right, right, 0),
        (0, 34, has_left, left, 1), (16, 35, has_left, left, 1),
    ):
        give((i == row) & given_to, column, group, sem)

    row_sel[...] = row_halo_selector(core)
    perm[...] = lane_permutation()
    edge_sel[...] = edge_selector()
    for n, da in enumerate((0, -1, 1)):
        near_sel[n] = near_selector(da)
        far_sel[n] = far_selector(da)
    shifted[:, 4:6] = jnp.zeros((4, 2, 16, 3 * D), BF16)
    near[36:48] = jnp.zeros((12, 8, D), BF16)
    far[9:16] = jnp.zeros((7, 8, D), BF16)

    @pl.when(jnp.logical_not(has_left))
    def _():
        near[32:34] = jnp.zeros((2, 8, D), BF16)

    @pl.when(jnp.logical_not(has_right))
    def _():
        near[34:36] = jnp.zeros((2, 8, D), BF16)

    @pl.loop(3, 6)
    def _(q):
        prepare(q)

    drain(send1, recv1, N_ROW - 1, 0).wait_send()
    drain(send2, near, N_ROW - 1, 1).wait_recv()

    def given(count, group, sem):
        return pltpu.make_async_remote_copy(
            src_ref=send2.at[pl.ds(0, count)], dst_ref=near.at[pl.ds(group, count)],
            send_sem=halo_send_sem.at[sem], recv_sem=halo_recv_sem.at[sem],
            device_id=(lax.rem(i + 1, N_ROW), k), device_id_type=MESH,
        )

    @pl.when(has_left)
    def _():
        given(2, 32, 0).wait_recv()

    @pl.when(has_right)
    def _():
        given(2, 34, 1).wait_recv()

    gathered = near[...].astype(F32).reshape(384, D).astype(BF16)
    row_halo[...] = dot(row_sel[...], gathered).reshape(10, 8, D).astype(BF16)
    row_copy = pltpu.make_async_remote_copy(
        src_ref=row_halo.at[pl.ds(0, 9)], dst_ref=far.at[pl.ds(0, 9)],
        send_sem=halo_send_sem.at[2], recv_sem=halo_recv_sem.at[2],
        device_id=(partner, k), device_id_type=MESH,
    )
    row_copy.start()

    for n in range(3):
        picked = dot(near_sel[n], gathered).reshape(4, 4, 16, D).astype(BF16)
        shifted[:, 1:4, :, n * D : (n + 1) * D] = picked[:, 0:3]
        shifted[:, pl.ds(4 * core, 1), :, n * D : (n + 1) * D] = picked[:, 3:4]
    lane = iota((1, 256), 1)

    def from_below(values):
        return jnp.where(lane >= 64, pltpu.roll(values.reshape(-1, 256), 64, 1), 0.0).reshape(values.shape)

    def from_above(values):
        return jnp.where(lane < 192, pltpu.roll(values.reshape(-1, 256), 192, 1), 0.0).reshape(values.shape)

    found = dot_nt(main_w[...].reshape(-1, D), shifted[:, 1:5, :, :D].reshape(256, D)).reshape(4, 8, 12, 8, 256)
    acc[...] = found[:, :, 2:10]
    acc[:, :, 0:2] += from_below(found[:, :, 10:12])
    acc[:, :, 6:8] += from_above(found[:, :, 0:2])
    for side in range(2):
        token_part = shifted[:, 1:5, :, (side + 1) * D : (side + 2) * D].reshape(256, D)
        found = dot_nt(side_w[side].reshape(-1, D), token_part).reshape(4, 2, 12, 8, 256)
        rows = pl.ds(6 * side, 2)
        acc[:, rows] += found[:, :, 2:10]
        acc[:, rows, 0:2] += from_below(found[:, :, 10:12])
        acc[:, rows, 6:8] += from_above(found[:, :, 0:2])

    drain(send2, near, N_ROW - 1, 1).wait_send()
    for present, sem in ((gives_right, 0), (gives_left, 1)):
        @pl.when(present)
        def _():
            given(N_ROW, 0, sem).wait_send()

    row_copy.wait()

    gathered = far[...].astype(F32).reshape(128, D).astype(BF16)
    for n in range(3):
        picked = dot(far_sel[n], gathered).reshape(4, 1, 16, D).astype(BF16)
        shifted[:, pl.ds(4 - 4 * core, 1), :, n * D : (n + 1) * D] = picked

    for side in range(2):
        token_part = shifted[:, 2 * side : 2 * side + 4].reshape(256, 3 * D)
        found = dot_nt(edge_w[side].reshape(-1, 3 * D), token_part).reshape(4, 12, 16, 256)
        edge_acc[:, :, side] = found[:, 2:10]
        edge_acc[:, 0:2, side] += from_below(found[:, 10:12])
        edge_acc[:, 6:8, side] += from_above(found[:, 0:2])

    solid = solid_ref[...]
    insides = [iota((8, 24, 128), 0) + 8 * h < solid[None] for h in range(4)]
    for first_c in range(0, 4, 2):
        lines = []
        for c in range(first_c, first_c + 2):
            edges = edge_acc[c].reshape(256, 256).astype(BF16)
            total = acc[c].reshape(512, 256) + dot(edge_sel[...], edges)
            for b in range(2):
                lines.append(jnp.concatenate(
                    [total[y * 64 : (y + 1) * 64, b * 128 : (b + 1) * 128] for y in range(8)], axis=1
                ))
        cells = dot(jnp.concatenate(lines, axis=0).astype(BF16), perm[...])
        for n in range(2):
            for h in range(4):
                b, low = h // 2, h % 2
                part = cells[128 * n + b * 64 : 128 * n + (b + 1) * 64]
                part = jnp.concatenate(
                    [part[:, low * 384 + r * 128 : low * 384 + (r + 1) * 128].reshape(8, 8, 128) for r in range(3)], axis=1
                )
                out_ref[first_c + n, 8 * h : 8 * h + 8] = jnp.where(insides[h], 0.0, part).astype(BF16)


def body(tokens, ln_gain, w_qkv, w_out, w_rec, solid_top):
    vmem = pl.BlockSpec(memory_space=pltpu.VMEM)
    hbm = pl.BlockSpec(memory_space=pltpu.HBM)
    return pl.pallas_call(
        kernel,
        out_shape=jax.ShapeDtypeStruct((4, 32, 24, 128), BF16),
        in_specs=[hbm] * 6,
        out_specs=vmem,
        scratch_shapes=[
            pltpu.VMEM((3, 16, 4, D), BF16),
            pltpu.VMEM((1, D), F32),
            pltpu.VMEM((24, 128), I32),
            pltpu.VMEM((D, 3 * D), BF16),
            pltpu.VMEM((D, D), BF16),
            pltpu.VMEM((D, 6912), BF16),
            pltpu.VMEM((32, 8, D), BF16),
            pltpu.VMEM((32, 8, D), BF16),
            pltpu.VMEM((32, 8, D), BF16),
            pltpu.VMEM((48, 8, D), BF16),
            pltpu.VMEM((16, 8, D), BF16),
            pltpu.VMEM((10, 8, D), BF16),
            pltpu.VMEM((8, 192, 256), BF16),
            pltpu.VMEM((4, 8, 6, 16, D), BF16),
            pltpu.VMEM((2, 4, 2, 6, 16, D), BF16),
            pltpu.VMEM((2, 4, 12, 16, 3 * D), BF16),
            pltpu.VMEM((3, 256, 384), BF16),
            pltpu.VMEM((3, 64, 128), BF16),
            pltpu.VMEM((1024, 768), BF16),
            pltpu.VMEM((512, 256), BF16),
            pltpu.VMEM((80, 384), BF16),
            pltpu.VMEM((256, 256), BF16),
            pltpu.VMEM((4, 6, 16, 3 * D), BF16),
            pltpu.VMEM((4, 8, 8, 8, 256), F32),
            pltpu.VMEM((4, 8, 2, 16, 256), F32),
            pltpu.VMEM((2, 4, 64, 1024), BF16),
            pltpu.SemaphoreType.DMA((11,)),
            pltpu.SemaphoreType.DMA((2,)),
            pltpu.SemaphoreType.DMA((2,)),
            pltpu.SemaphoreType.DMA((4,)),
            pltpu.SemaphoreType.DMA((4,)),
        ],
        compiler_params=pltpu.CompilerParams(
            collective_id=0, has_side_effects=True, vmem_limit_bytes=60 * 1024 * 1024
        ),
        cost_estimate=pl.CostEstimate(flops=6 * 10**9, bytes_accessed=11 * 10**6, transcendentals=2**19),
        name="airflow_block",
    )(tokens, ln_gain.reshape(1, D), w_qkv, w_out, w_rec, solid_top)


def solution(mesh):
    in_specs = (P("row", "aisle", None, None), P(), P(), P(), P(), P("row", "aisle"))
    out_specs = P(None, None, "row", "aisle")
    return jax.shard_map(body, mesh=mesh, in_specs=in_specs, out_specs=out_specs, check_vma=False)
```

```python
import jax
import jax.numpy as jnp
from jax import lax
from jax.experimental import pallas as pl
from jax.experimental.pallas import tpu as pltpu
from jax.sharding import PartitionSpec as P

EPSILON = 1e-05
N_ROW, N_AISLE = 32, 8
D, HEADS, DH = 512, 8, 64
MESH = pl.DeviceIdType.MESH
F32, BF16, I32 = jnp.float32, jnp.bfloat16, jnp.int32


def iota(shape, dim):
    return lax.broadcasted_iota(I32, shape, dim)


def one_hot(hit):
    return jnp.where(hit, 1.0, 0.0).astype(BF16)


def dot(a, b):
    return lax.dot_general(a, b, (((1,), (0,)), ((), ())), preferred_element_type=F32)


def dot_nt(a, b):
    return lax.dot_general(a, b, (((1,), (1,)), ((), ())), preferred_element_type=F32)


def send_selector():
    row = iota((256, 1), 0)
    pair = ((row >> 3) & 15) * 2 + (row >> 7)
    source = (row & 3) * 64 + pair * 2 + ((row >> 2) & 1)
    source = jnp.where((row & 3) < 3, source, -1)
    return one_hot(iota((256, 192), 1) == source)


def weight_selector(step):
    row = iota((192, 1), 0)
    main = ((row & 7) + 2) * 12 + (row >> 3) + 2
    below = ((row & 7) + 2) * 12 + ((row >> 3) & 1) + 10
    above = ((row & 7) + 2) * 12 + ((row >> 3) & 1)
    edge = row - 96
    side = jnp.where(edge >= 48, 1, 0)
    edge = edge - 48 * side
    part = edge >> 4
    y = (edge >> 1) & 7
    x = edge & 1
    kx = jnp.where(side == 0, x + 10, x)
    ky = jnp.where(
        part == 0,
        y + 2,
        jnp.where(
            part == 1, jnp.where(y < 2, y + 10, -999), jnp.where(y >= 6, y - 6, -999)
        ),
    )
    edged = kx * 12 + ky
    column = jnp.where(row < 64, main, jnp.where(row < 80, below, jnp.where(row < 96, above, edged)))
    return one_hot(iota((192, 256), 1) - 16 * step == column)


def near_selector(da):
    q = iota((256, 1), 0)
    h, r, a = q >> 6, (q >> 4) & 3, (q & 15) + da
    block = jnp.where(a < 0, 16, jnp.where(a > 15, 17, a))
    return one_hot(iota((256, 384), 1) == block * 16 + h * 4 + r)


def far_selector(da):
    q = iota((64, 1), 0)
    h, a = q >> 4, (q & 15) + da
    block = jnp.where(a < 0, 16, jnp.where(a > 15, 17, a))
    return one_hot(iota((64, 128), 1) == block * 4 + h)


def slot_selector():
    row = iota((256, 1), 0)
    i, slot = row >> 3, row & 3
    beside = jnp.where((i & 1) == 0, row - 9, row + 5)
    beside = jnp.where((i == 0) | (i == N_ROW - 1), -1, beside)
    return one_hot(iota((256, 256), 1) == jnp.where(slot < 3, row, beside))


def lane_permutation():
    row = iota((1024, 1), 0)
    r = (row >> 4) & 3
    target = ((row >> 6) & 1) * 384 + r * 128 + (row & 15) * 8 + (row >> 7)
    target = jnp.where(r < 3, target, -1)
    return one_hot(iota((1024, 768), 1) == target)


def edge_selector():
    column = iota((1, 256), 1)
    target = (
        ((column >> 1) & 7) * 64 + (column >> 5) * 8 + ((column >> 4) & 1) * 6 + (column & 1)
    )
    return one_hot(iota((512, 256), 0) == target)


def row_halo_selector(core):
    row = iota((80, 1), 0)
    source = jnp.where(row < 72, row * 4 + 2 - 2 * core, -1)
    return one_hot(iota((80, 384), 1) == source)


def attend_lines(x, gain, w_qkv, w_out):
    center = x - jnp.mean(x, axis=-1, keepdims=True)
    spread = jnp.mean(center * center, axis=-1, keepdims=True)
    normed = (center * lax.rsqrt(spread + EPSILON) * gain).astype(BF16)
    qkv = dot(normed, w_qkv).astype(BF16)
    rows, cols = iota((256, 256), 0), iota((256, 256), 1)
    valid = (((rows ^ cols) & 4) == 0) & ((cols & 3) < 3)
    first = iota((256, 128), 1) < DH
    mask_first = one_hot(first)
    mask_second = 1 - mask_first
    parts = []
    for pair in range(HEADS // 2):
        at = pair * 2 * DH
        query = qkv[:, at : at + 2 * DH]
        key = qkv[:, D + at : D + at + 2 * DH]
        value = qkv[:, 2 * D + at : 2 * D + at + 2 * DH]
        halves = []
        for mask in (mask_first, mask_second):
            scores = dot_nt(query * mask, key) * (1.0 / 8.0)
            scores = jnp.where(valid, scores, -jnp.inf)
            grown = jnp.exp(scores - jnp.max(scores, axis=-1, keepdims=True))
            total = jnp.sum(grown, axis=-1, keepdims=True)
            halves.append(dot(grown.astype(BF16), value) / total)
        parts.append(jnp.where(first, halves[0], halves[1]).astype(BF16))
    attended = jnp.concatenate(parts, axis=1)
    return x + dot(attended, w_out)


def kernel(
    tokens_hbm, gain_hbm, w_qkv_hbm, w_out_hbm, w_rec_hbm, solid_hbm,
    out_ref,
    tokens, gain, solid_ref, w_qkv, w_out, w_rec, send1, recv1, send2, near, far, row_halo,
    w_sel, main_w, side_w, edge_w, near_sel, far_sel, perm, edge_sel, row_sel, slot_sel,
    shifted, acc, edge_acc, ready,
    load_sem, send_sem, recv_sem, halo_send_sem, halo_recv_sem, store_sem, cells_v,
):
    i, k = lax.axis_index("row"), lax.axis_index("aisle")

    token_load = pltpu.make_async_copy(tokens_hbm, tokens, load_sem.at[6])
    token_load.start()
    loads = [
        pltpu.make_async_copy(gain_hbm, gain, load_sem.at[7]),
        pltpu.make_async_copy(w_qkv_hbm, w_qkv, load_sem.at[8]),
        pltpu.make_async_copy(w_out_hbm, w_out, load_sem.at[9]),
        pltpu.make_async_copy(solid_hbm, solid_ref, load_sem.at[10]),
    ]
    for load in loads:
        load.start()

    def rec_load(q):
        columns = pl.ds(pl.multiple_of(q * 1152, 1152), 1152)
        return pltpu.make_async_copy(w_rec_hbm.at[:, columns], w_rec.at[:, columns], load_sem.at[q])

    for q in range(6):
        rec_load(q).start()

    barrier = pltpu.get_barrier_semaphore()
    core = lax.rem(i, 2)
    partner = i + 1 - 2 * core
    right, left = lax.rem(k + 1, N_AISLE), lax.rem(k + N_AISLE - 1, N_AISLE)
    has_right, has_left = k < N_AISLE - 1, k > 0
    pair = lax.rem(i, 16) * 2 + lax.div(i, 16)
    gives_left, gives_right = (lax.rem(i, 16) == 0) & has_left, (lax.rem(i, 16) == 15) & has_right

    @pl.loop(1, N_ROW)
    def _(step):
        pl.semaphore_signal(barrier, inc=1, device_id=(lax.rem(i + step, N_ROW), k), device_id_type=MESH)

    for present, column, first in ((has_left, left, 15), (has_right, right, 0)):
        @pl.when(present)
        def _():
            for j in (first, first + 16):
                pl.semaphore_signal(barrier, inc=1, device_id=(j, column), device_id_type=MESH)

    token_load.wait()
    mine = tokens[...].astype(F32).reshape(192, D).astype(BF16)
    send1[...] = dot(send_selector(), mine).reshape(32, 8, D).astype(BF16)
    recv1[i] = send1[i]
    pl.semaphore_wait(barrier, N_ROW - 1 + N_ROW * (gives_left.astype(I32) + gives_right.astype(I32)))

    def exchange(source, target, place, sem):
        @pl.loop(1, N_ROW)
        def _(step):
            j = lax.rem(i + step, N_ROW)
            pltpu.make_async_remote_copy(
                src_ref=source.at[j], dst_ref=target.at[place],
                send_sem=send_sem.at[sem], recv_sem=recv_sem.at[sem],
                device_id=(j, k), device_id_type=MESH,
            ).start()

    def drain(source, target, count, sem, start=0):
        return pltpu.make_async_remote_copy(
            src_ref=source.at[pl.ds(start, count)], dst_ref=target.at[pl.ds(start, count)],
            send_sem=send_sem.at[sem], recv_sem=recv_sem.at[sem],
            device_id=(lax.rem(i + 1, N_ROW), k), device_id_type=MESH,
        )

    exchange(send1, recv1, i, 0)

    @pl.loop(0, 8)
    def _(s):
        w_sel[s] = weight_selector(s)

    def prepare(q):
        rec_load(q).wait()
        for p in range(4):
            index = q * 4 + p
            c, pair = index // 6, index % 6
            found = []
            for s in (2 * p, 2 * p + 1):
                window = w_rec[:, pl.ds(pl.multiple_of(128 * (9 * q + s), 128), 256)]
                found.append(dot_nt(w_sel[s], window))
            main = [f[:64].reshape(8, 8, D) for f in found]
            main_w[c, :, pair] = jnp.concatenate(main, axis=1).astype(BF16)
            for side in range(2):
                at = 64 + 16 * side
                halves = [f[at : at + 16].reshape(2, 8, D) for f in found]
                side_w[side, c, :, pair] = jnp.concatenate(halves, axis=1).astype(BF16)
                for n in range(2):
                    for part in range(3):
                        at = 96 + 48 * side + 16 * part
                        edge_w[side, c, 2 * pair + n, :, part * D : (part + 1) * D] = found[n][at : at + 16].astype(BF16)

    slot_sel[...] = slot_selector()

    @pl.loop(0, 3)
    def _(q):
        prepare(q)

    for load in loads:
        load.wait()
    drain(send1, recv1, N_ROW - 1, 0).wait_recv()

    x = recv1[...].astype(F32).reshape(256, D)
    block_out = attend_lines(x, gain[...], w_qkv[...], w_out[...])
    send2[...] = dot(slot_sel[...], block_out.astype(BF16)).reshape(32, 8, D).astype(BF16)
    near[pair] = send2[i]

    def give(present, column, group, sem):
        @pl.when(present)
        def _():
            @pl.loop(0, N_ROW)
            def _(step):
                j = lax.rem(i + step, N_ROW)
                pltpu.make_async_remote_copy(
                    src_ref=send2.at[j], dst_ref=near.at[group],
                    send_sem=halo_send_sem.at[sem], recv_sem=halo_recv_sem.at[sem],
                    device_id=(j, column), device_id_type=MESH,
                ).start()

    exchange(send2, near, pair, 1)
    for row, group, given_to, column, sem in (
        (15, 32, has_right, right, 0), (31, 33, has_right, right, 0),
        (0, 34, has_left, left, 1), (16, 35, has_left, left, 1),
    ):
        give((i == row) & given_to, column, group, sem)

    row_sel[...] = row_halo_selector(core)
    perm[...] = lane_permutation()
    edge_sel[...] = edge_selector()
    for n, da in enumerate((0, -1, 1)):
        near_sel[n] = near_selector(da)
        far_sel[n] = far_selector(da)
    shifted[:, 4:6] = jnp.zeros((4, 2, 16, 3 * D), BF16)
    near[36:48] = jnp.zeros((12, 8, D), BF16)
    far[9:16] = jnp.zeros((7, 8, D), BF16)

    @pl.when(jnp.logical_not(has_left))
    def _():
        near[32:34] = jnp.zeros((2, 8, D), BF16)

    @pl.when(jnp.logical_not(has_right))
    def _():
        near[34:36] = jnp.zeros((2, 8, D), BF16)

    @pl.loop(3, 6)
    def _(q):
        prepare(q)

    drain(send1, recv1, N_ROW - 1, 0).wait_send()
    drain(send2, near, N_ROW - 1, 1).wait_recv()

    def given(count, group, sem):
        return pltpu.make_async_remote_copy(
            src_ref=send2.at[pl.ds(0, count)], dst_ref=near.at[pl.ds(group, count)],
            send_sem=halo_send_sem.at[sem], recv_sem=halo_recv_sem.at[sem],
            device_id=(lax.rem(i + 1, N_ROW), k), device_id_type=MESH,
        )

    @pl.when(has_left)
    def _():
        given(2, 32, 0).wait_recv()

    @pl.when(has_right)
    def _():
        given(2, 34, 1).wait_recv()

    gathered = near[...].astype(F32).reshape(384, D).astype(BF16)
    row_halo[...] = dot(row_sel[...], gathered).reshape(10, 8, D).astype(BF16)
    row_copy = pltpu.make_async_remote_copy(
        src_ref=row_halo.at[pl.ds(0, 9)], dst_ref=far.at[pl.ds(0, 9)],
        send_sem=halo_send_sem.at[2], recv_sem=halo_recv_sem.at[2],
        device_id=(partner, k), device_id_type=MESH,
    )
    row_copy.start()

    for n in range(3):
        picked = dot(near_sel[n], gathered).reshape(4, 4, 16, D).astype(BF16)
        shifted[:, 1:4, :, n * D : (n + 1) * D] = picked[:, 0:3]
        shifted[:, pl.ds(4 * core, 1), :, n * D : (n + 1) * D] = picked[:, 3:4]
    lane = iota((1, 256), 1)

    def from_below(values):
        return jnp.where(lane >= 64, pltpu.roll(values.reshape(-1, 256), 64, 1), 0.0).reshape(values.shape)

    def from_above(values):
        return jnp.where(lane < 192, pltpu.roll(values.reshape(-1, 256), 192, 1), 0.0).reshape(values.shape)

    found = dot_nt(main_w[...].reshape(-1, D), shifted[:, 1:5, :, :D].reshape(256, D)).reshape(4, 8, 12, 8, 256)
    acc[...] = found[:, :, 2:10]
    acc[:, :, 0:2] += from_below(found[:, :, 10:12])
    acc[:, :, 6:8] += from_above(found[:, :, 0:2])
    for side in range(2):
        token_part = shifted[:, 1:5, :, (side + 1) * D : (side + 2) * D].reshape(256, D)
        found = dot_nt(side_w[side].reshape(-1, D), token_part).reshape(4, 2, 12, 8, 256)
        rows = pl.ds(6 * side, 2)
        acc[:, rows] += found[:, :, 2:10]
        acc[:, rows, 0:2] += from_below(found[:, :, 10:12])
        acc[:, rows, 6:8] += from_above(found[:, :, 0:2])

    drain(send2, near, N_ROW - 1, 1).wait_send()
    for present, sem in ((gives_right, 0), (gives_left, 1)):
        @pl.when(present)
        def _():
            given(N_ROW, 0, sem).wait_send()

    row_copy.wait()

    gathered = far[...].astype(F32).reshape(128, D).astype(BF16)
    for n in range(3):
        picked = dot(far_sel[n], gathered).reshape(4, 1, 16, D).astype(BF16)
        shifted[:, pl.ds(4 - 4 * core, 1), :, n * D : (n + 1) * D] = picked

    for side in range(2):
        token_part = shifted[:, 2 * side : 2 * side + 4].reshape(256, 3 * D)
        found = dot_nt(edge_w[side].reshape(-1, 3 * D), token_part).reshape(4, 12, 16, 256)
        edge_acc[:, :, side] = found[:, 2:10]
        edge_acc[:, 0:2, side] += from_below(found[:, 10:12])
        edge_acc[:, 6:8, side] += from_above(found[:, 0:2])

    solid = solid_ref[...]
    insides = [iota((8, 24, 128), 0) + 8 * h < solid[None] for h in range(4)]
    for first_c in range(0, 4, 2):
        lines = []
        for c in range(first_c, first_c + 2):
            edges = edge_acc[c].reshape(256, 256).astype(BF16)
            total = acc[c].reshape(512, 256) + dot(edge_sel[...], edges)
            for b in range(2):
                lines.append(jnp.concatenate(
                    [total[y * 64 : (y + 1) * 64, b * 128 : (b + 1) * 128] for y in range(8)], axis=1
                ))
        cells = dot(jnp.concatenate(lines, axis=0).astype(BF16), perm[...])
        for n in range(2):
            for h in range(4):
                b, low = h // 2, h % 2
                part = cells[128 * n + b * 64 : 128 * n + (b + 1) * 64]
                part = jnp.concatenate(
                    [part[:, low * 384 + r * 128 : low * 384 + (r + 1) * 128].reshape(8, 8, 128) for r in range(3)], axis=1
                )
                cells_v[first_c + n, 8 * h : 8 * h + 8] = jnp.where(insides[h], 0.0, part).astype(BF16)
            pltpu.make_async_copy(cells_v.at[first_c + n], out_ref.at[first_c + n], store_sem.at[first_c + n]).start()
    for c in range(4):
        pltpu.make_async_copy(cells_v.at[c], out_ref.at[c], store_sem.at[c]).wait()


def body(tokens, ln_gain, w_qkv, w_out, w_rec, solid_top):
    hbm = pl.BlockSpec(memory_space=pltpu.HBM)
    return pl.pallas_call(
        kernel,
        out_shape=jax.ShapeDtypeStruct((4, 32, 24, 128), BF16),
        in_specs=[hbm] * 6,
        out_specs=hbm,
        scratch_shapes=[
            pltpu.VMEM((3, 16, 4, D), BF16),
            pltpu.VMEM((1, D), F32),
            pltpu.VMEM((24, 128), I32),
            pltpu.VMEM((D, 3 * D), BF16),
            pltpu.VMEM((D, D), BF16),
            pltpu.VMEM((D, 6912), BF16),
            pltpu.VMEM((32, 8, D), BF16),
            pltpu.VMEM((32, 8, D), BF16),
            pltpu.VMEM((32, 8, D), BF16),
            pltpu.VMEM((48, 8, D), BF16),
            pltpu.VMEM((16, 8, D), BF16),
            pltpu.VMEM((10, 8, D), BF16),
            pltpu.VMEM((8, 192, 256), BF16),
            pltpu.VMEM((4, 8, 6, 16, D), BF16),
            pltpu.VMEM((2, 4, 2, 6, 16, D), BF16),
            pltpu.VMEM((2, 4, 12, 16, 3 * D), BF16),
            pltpu.VMEM((3, 256, 384), BF16),
            pltpu.VMEM((3, 64, 128), BF16),
            pltpu.VMEM((1024, 768), BF16),
            pltpu.VMEM((512, 256), BF16),
            pltpu.VMEM((80, 384), BF16),
            pltpu.VMEM((256, 256), BF16),
            pltpu.VMEM((4, 6, 16, 3 * D), BF16),
            pltpu.VMEM((4, 8, 8, 8, 256), F32),
            pltpu.VMEM((4, 8, 2, 16, 256), F32),
            pltpu.VMEM((2, 4, 64, 1024), BF16),
            pltpu.SemaphoreType.DMA((11,)),
            pltpu.SemaphoreType.DMA((2,)),
            pltpu.SemaphoreType.DMA((2,)),
            pltpu.SemaphoreType.DMA((4,)),
            pltpu.SemaphoreType.DMA((4,)),
            pltpu.SemaphoreType.DMA((4,)),
            pltpu.VMEM((4, 32, 24, 128), BF16),
        ],
        compiler_params=pltpu.CompilerParams(
            collective_id=0, has_side_effects=True, vmem_limit_bytes=60 * 1024 * 1024
        ),
        cost_estimate=pl.CostEstimate(flops=6 * 10**9, bytes_accessed=11 * 10**6, transcendentals=2**19),
        name="airflow_block",
    )(tokens, ln_gain.reshape(1, D), w_qkv, w_out, w_rec, solid_top)


def solution(mesh):
    in_specs = (P("row", "aisle", None, None), P(), P(), P(), P(), P("row", "aisle"))
    out_specs = P(None, None, "row", "aisle")
    return jax.shard_map(body, mesh=mesh, in_specs=in_specs, out_specs=out_specs, check_vma=False)
```
